256 devices in a mesh: owner: 16 (over y, x), tp: 16 (over z, core).
Axes of the slice: x: 4, y: 4, z: 8, core: 2. Of those that a mesh axis runs over, the one named last changes fastest.
Arguments:
- queries: bfloat16 [2048, 8192], P('owner', 'tp'), may hold values from -200 to 200
- out_grad: bfloat16 [2048, 8192], P('owner', 'tp'), may hold values from -12 to 12
- own_kv: bfloat16 [2048, 16, 128], P('owner', 'tp'), may hold values from -6 to 6
- passage_kv: bfloat16 [256, 16, 256, 128], P('owner', 'tp'), may hold values from -8 to 8
- query_weight: bfloat16 [8192, 8192], P(None, 'tp'), may hold values from -0.0625 to 0.0625
- retrieval: int32 [16, 16], replicated, may hold values from 0 to 255, as said below
- passage_slot: int32 [256], replicated, may hold values from 0 to 255, as said below
- passage_blocks: int32 [256], replicated, may hold values from 1 to 2
Outputs:
- grad_input: bfloat16 [2048, 8192], P(('owner', 'tp'))
- passage_grad: bfloat16 [256, 16, 256, 128], P('owner', 'tp')
- own_grad: bfloat16 [2048, 16, 128], P('owner', 'tp')
The draws below stay inside these ranges and needn't reach their ends.
Inputs may be any that keep to these rules, and one draw needn't show every extreme that they name: `retrieval`: each row names 16 distinct passage ids. Passage p lies in cache slot passage_slot[p], on owner index passage_slot[p] // 16; at most 2 passages of one row lie on one owner index, and in every row some owner index holds exactly 2 of them. `passage_slot`: A permutation of the cache slots.
All inputs are finite; a program needn't handle non-finite values.
Results may differ from the reference program's by a relative error of at most 0.022.
Values may be sent and summed in bfloat16 or wider, within the bound.
A program may use at most 128 MiB of HBM per device.

```python
import jax
import jax.numpy as jnp
from jax import lax

D = 8192
HS = 128
H_DEV = 4
TOK_DEV = 128
RETR = 16
PLEN = 256
BLK = 128
P_DEV = 16
HEADS = 64
KV_HEADS = 8
GROUP = 8
CAP = 2
SEQS = 16
TOKENS = 2048
PASSAGES = 256
N_TP = 16


def owner_layout(key):
    perm_key, pick_key = jax.random.split(key, 2)
    passage_slot = jax.random.permutation(perm_key, PASSAGES).astype(jnp.int32)
    slot_passage = jnp.argsort(passage_slot).astype(jnp.int32)
    owner_total = PASSAGES // P_DEV
    entry_total = owner_total * CAP
    entry_owner = jnp.arange(entry_total, dtype=jnp.int32) // CAP
    entry_copy = jnp.arange(entry_total, dtype=jnp.int32) % CAP

    def one_sequence(row_key):
        full_key, order_key, local_key, shuffle_key = jax.random.split(row_key, 4)
        full_owner = jax.random.randint(full_key, (), 0, owner_total)
        priority = jax.random.permutation(order_key, entry_total).astype(jnp.int32)
        priority = jnp.where(entry_owner == full_owner, entry_copy - CAP, priority)
        chosen = jnp.argsort(priority)[:RETR]
        chosen_owner = entry_owner[chosen]
        chosen_copy = entry_copy[chosen]
        local_order = jax.vmap(lambda sub_key: jax.random.permutation(sub_key, P_DEV))(jax.random.split(local_key, owner_total))
        local_slot = local_order[chosen_owner, chosen_copy].astype(jnp.int32)
        picked = slot_passage[chosen_owner * P_DEV + local_slot]
        return picked[jax.random.permutation(shuffle_key, RETR)]
    retrieval = jax.vmap(one_sequence)(jax.random.split(pick_key, SEQS)).astype(jnp.int32)
    return (passage_slot, retrieval)


def cache_values(key):
    return jax.random.normal(jax.random.fold_in(key, 11), (PASSAGES, N_TP, PLEN, HS), jnp.float32)


def draw_retrieval(key, part):
    return owner_layout(key)[1]


def draw_passage_slot(key, part):
    return owner_layout(key)[0]


def draw_passage_kv(key, part):
    base_draw = cache_values(key)
    return base_draw.astype(jnp.bfloat16)


def draw_queries(key, part):
    key = jax.random.fold_in(key, 5)
    return (2.0 * jax.random.normal(key, (TOKENS, HEADS * HS), jnp.float32)).astype(jnp.bfloat16)


def place_ends(result, stream_key, least, top_value):
    extent = result.shape
    index_at = [jax.random.randint(jax.random.fold_in(stream_key, axis), (), 0, extent[axis]) for axis in range(len(extent))]
    result = result.at[tuple(index_at)].set(least)
    longest = extent.index(max(extent))
    index_at[longest] = (index_at[longest] + 1) % extent[longest]
    return result.at[tuple(index_at)].set(top_value)


def shard_levels(key, extent, shards, least, high):
    def one(axis_at, parts):
        heights = jax.random.uniform(jax.random.fold_in(jax.random.fold_in(key, 6), axis_at), (parts,), jnp.float32, least / len(shards), high / len(shards))
        return jnp.repeat(jnp.exp(heights), extent[axis_at] // parts).reshape((-1,) + (1,) * (len(extent) - axis_at - 1))

    gain = one(*shards[0])
    for cut in shards[1:]:
        gain = gain * one(*cut)
    return gain


def noise(rng, shape, spread, most, cuts=(), held_as=jnp.bfloat16):
    drawn = spread * jax.random.normal(rng, shape, jnp.float32)
    if cuts:
        drawn = drawn * shard_levels(rng, shape, cuts, -0.22, 0.18)
    return jnp.clip(drawn, -most, most).astype(held_as)


def setup_inputs(seed: int = 0) -> dict:
    splits = jax.random.split(jax.random.key(seed), 9)
    return {
        "queries": draw_queries(jax.random.fold_in(splits[8], 71), 0),
        "out_grad": noise(splits[1], (TOKENS, HEADS * HS), 2.0, 12.0, ((0, 16), (1, 16))),
        "own_kv": noise(splits[2], (TOKENS, N_TP, HS), 1.0, 6.0, ((0, 16), (1, 16))),
        "passage_kv": draw_passage_kv(jax.random.fold_in(splits[8], 71), 0),
        "query_weight": noise(splits[4], (D, HEADS * HS), (HEADS * HS) ** -0.5, 0.0625, ((1, 16),)),
        "retrieval": draw_retrieval(jax.random.fold_in(splits[8], 71), 0),
        "passage_slot": draw_passage_slot(jax.random.fold_in(splits[8], 71), 0),
        "passage_blocks": place_ends(jax.random.randint(splits[7], (PASSAGES,), 1, PLEN // BLK + 1), jax.random.fold_in(splits[7], 1), 1, (PLEN // BLK + 1) - 1).astype(jnp.int32),
    }


MASKED_SCORE = -1e30


def sequence_grads(query_rows, grad_rows, own_rows, passage_rows, live_cols):
    score_scale = HS ** -0.5
    passage_len = RETR * PLEN
    causal = jnp.arange(TOK_DEV)[None, :] <= jnp.arange(TOK_DEV)[:, None]
    visible = jnp.concatenate([jnp.broadcast_to(live_cols[None, :], (TOK_DEV, passage_len)), causal], axis=1)
    dq_list = []
    grad_list = []
    for kv_group in range(KV_HEADS):
        key_rows = jnp.concatenate([passage_rows[:, 2 * kv_group].reshape(passage_len, HS), own_rows[:, 2 * kv_group]], axis=0).astype(jnp.float32)
        value_rows = jnp.concatenate([passage_rows[:, 2 * kv_group + 1].reshape(passage_len, HS), own_rows[:, 2 * kv_group + 1]], axis=0).astype(jnp.float32)
        first_head = kv_group * GROUP
        query_block = query_rows[:, first_head:first_head + GROUP].astype(jnp.float32)
        grad_block = grad_rows[:, first_head:first_head + GROUP].astype(jnp.float32)
        scores = jnp.einsum("thd,kd->htk", query_block, key_rows) * score_scale
        scores = jnp.where(visible[None], scores, MASKED_SCORE)
        row_max = jnp.max(scores, axis=-1, keepdims=True)
        exp_rows = jnp.exp(scores - row_max)
        prob_rows = exp_rows / jnp.sum(exp_rows, axis=-1, keepdims=True)
        prob_b = prob_rows.astype(jnp.bfloat16).astype(jnp.float32)
        outputs = jnp.einsum("htk,kd->thd", prob_b, value_rows)
        row_delta = jnp.sum(grad_block * outputs, axis=-1)
        prob_grad = jnp.einsum("thd,kd->htk", grad_block, value_rows)
        dscore = (prob_rows * (prob_grad - jnp.transpose(row_delta)[:, :, None]) * score_scale).astype(jnp.bfloat16)
        dscore_f = dscore.astype(jnp.float32)
        dq_list.append(jnp.einsum("htk,kd->thd", dscore_f, key_rows).astype(jnp.bfloat16))
        key_grad = jnp.einsum("htk,thd->kd", dscore_f, query_block)
        value_grad = jnp.einsum("htk,thd->kd", prob_b, grad_block)
        grad_list.append(jnp.stack([key_grad, value_grad], axis=0))
    dq_rows = jnp.concatenate(dq_list, axis=1)
    all_grads = jnp.stack(grad_list, axis=0).reshape(N_TP, passage_len + TOK_DEV, HS)
    passage_terms = jnp.transpose(all_grads[:, :passage_len].reshape(N_TP, RETR, PLEN, HS), (1, 0, 2, 3))
    own_terms = jnp.transpose(all_grads[:, passage_len:], (1, 0, 2))
    return dq_rows, passage_terms, own_terms


def reference(queries, out_grad, own_kv, passage_kv, query_weight, retrieval, passage_slot, passage_blocks):
    def one_sequence(inputs):
        query_rows, grad_rows, own_rows, passage_ids = inputs
        slots = passage_slot[passage_ids]
        passage_rows = passage_kv[slots]
        live_cols = (jnp.arange(PLEN)[None, :] < (passage_blocks[passage_ids] * BLK)[:, None]).reshape(RETR * PLEN)
        return sequence_grads(query_rows, grad_rows, own_rows, passage_rows, live_cols)

    dq_all, passage_all, own_all = lax.map(one_sequence, (queries.reshape(SEQS, TOK_DEV, HEADS, HS), out_grad.reshape(SEQS, TOK_DEV, HEADS, HS), own_kv.reshape(SEQS, TOK_DEV, N_TP, HS), retrieval))
    slots_all = passage_slot[retrieval].reshape(SEQS * RETR)
    passage_total = jnp.zeros((PASSAGES, N_TP, PLEN, HS), jnp.float32).at[slots_all].add(passage_all.reshape(SEQS * RETR, N_TP, PLEN, HS))
    passage_grad = passage_total.astype(jnp.bfloat16)
    own_grad = own_all.reshape(TOKENS, N_TP, HS).astype(jnp.bfloat16)
    dq_flat = dq_all.reshape(TOKENS, HEADS * HS)
    col_width = H_DEV * HS
    grad_total = jnp.zeros((TOKENS, D), jnp.float32)
    for tp_index in range(N_TP):
        lo_col = tp_index * col_width
        partial_value = jnp.dot(dq_flat[:, lo_col:lo_col + col_width], jnp.transpose(query_weight[:, lo_col:lo_col + col_width]), preferred_element_type=jnp.float32)
        grad_total = grad_total + lax.optimization_barrier(partial_value.astype(jnp.bfloat16)).astype(jnp.float32)
    grad_input = grad_total.astype(jnp.bfloat16)
    return grad_input, passage_grad, own_grad
```

```python
import functools
import math

import jax
import jax.numpy as jnp
from jax import lax
from jax.experimental import pallas as pl
from jax.experimental.pallas import tpu as pltpu
from jax.sharding import PartitionSpec as P

MESH = pl.DeviceIdType.MESH
BF = jnp.bfloat16
F32 = jnp.float32
MASKED = -1e30
OWN = 16
RET = 16
PLEN = 256
HS = 128
HD = 4
ROWS = 512
SCALE = HS ** -0.5
LOG2E = 1.0 / math.log(2.0)
CB = 8
CBW = 1024


def mm(a, b):
    return lax.dot_general(a, b, (((1,), (0,)), ((), ())), preferred_element_type=F32)


def fold(x, op):
    return op(x.reshape(x.shape[0] // 8, 8, x.shape[1]), axis=0)


def main_kernel(
    retr, pslot, pblk, q_ref, do_ref, own_ref, pkv_ref, w_ref,
    gi_ref, og_ref, ret_ref, tab_ref,
    kvl, ownx, snd, arrk, arrv, e_ref, eo_ref, dp_ref, dpo_ref, qs, qt, dos, dot_, dosn,
    dkv, dqt, give, got, sret, wv, zall, zgot, zsnd, zrcv, ogive, ogot,
    pos, inv, pre_s, pre_r, a_s, a_r, b_s, b_r, g_s, g_r, t_s, t_r, z_s, z_r, misc,
):
    o = lax.axis_index("owner")
    t = lax.axis_index("tp")
    c = lax.rem(t, 2)
    zi = t // 2
    mate = t + 1 - 2 * c

    arr = (arrk, arrv)

    def rcopy(src, dst, ss, rs, dev):
        return pltpu.make_async_remote_copy(
            src_ref=src, dst_ref=dst, send_sem=ss, recv_sem=rs, device_id=dev, device_id_type=MESH
        )

    load_kv = pltpu.make_async_copy(pkv_ref, kvl.at[c], misc.at[0])
    load_kv.start()
    load_w = pltpu.make_async_copy(w_ref, wv, misc.at[1])
    load_w.start()

    bar = pltpu.get_barrier_semaphore()

    def greet(i, _):
        s = lax.rem(o + i, OWN)
        pl.semaphore_signal(bar, inc=1, device_id=(s, t), device_id_type=MESH)
        pl.semaphore_signal(bar, inc=1, device_id=(s, mate), device_id_type=MESH)
        return 0

    lax.fori_loop(1, OWN, greet, 0)
    zup = lax.rem(zi + 1, 8) * 2 + c
    zdn = lax.rem(zi + 7, 8) * 2 + c
    for dev in (mate, zup, zdn):
        pl.semaphore_signal(bar, inc=1, device_id=(o, dev), device_id_type=MESH)

    def table(s, _):
        first = jnp.int32(-1)
        second = jnp.int32(-1)
        for j in range(RET):
            slot = pslot[retr[s, j]]
            hit = slot // OWN == o
            local = lax.rem(slot, OWN)
            second = jnp.where(hit & (first >= 0), local, second)
            first = jnp.where(hit & (first < 0), local, first)
        tab_ref[2 * s] = first
        tab_ref[2 * s + 1] = second
        return 0

    lax.fori_loop(0, OWN, table, 0)
    ownx[c] = own_ref[...]
    pl.semaphore_wait(bar, 33)

    own_x = rcopy(ownx.at[c], ownx.at[c], pre_s.at[1], pre_r.at[1], (o, mate))
    own_x.start()
    load_kv.wait()
    kv_x = rcopy(kvl.at[c], kvl.at[c], pre_s.at[0], pre_r.at[0], (o, mate))
    kv_x.start()

    owners = []
    ranks = []
    for j in range(RET):
        ow = pslot[retr[o, j]] // OWN
        rank = jnp.int32(0)
        for prev in owners:
            rank = rank + (prev == ow).astype(jnp.int32)
        rank = jnp.minimum(rank, 1)
        owners.append(ow)
        ranks.append(rank)
        pos[j] = rank * OWN + ow

    def inverse(n, _):
        at = jnp.int32(0)
        for j in range(RET):
            at = jnp.where(pos[j] == n, j, at)
        inv[n] = at
        return 0

    lax.fori_loop(0, 2 * OWN, inverse, 0)

    for h in range(HD):
        rows = pl.ds(h * 128, 128)
        qh = q_ref[:, h * 128:(h + 1) * 128]
        dh = do_ref[:, h * 128:(h + 1) * 128]
        qs[rows, :] = qh
        dos[rows, :] = dh
        qt[:, rows] = qh.T
        dot_[:, rows] = dh.T

    own_x.wait()
    kv_x.wait()

    def hop(k, i):
        s = lax.rem(o + i, OWN)
        return rcopy(
            snd.at[k, i], arr[k].at[c * OWN + o], a_s.at[k, i], a_r.at[k, o], (s, t)
        )

    def send_kind(k):
        def step(i, _):
            s = lax.rem(o + i, OWN)
            at = jnp.maximum(tab_ref[2 * s + c], 0)
            snd[k, i] = kvl[k, at]
            hop(k, i).start()
            return 0

        lax.fori_loop(1, OWN, step, 0)
        arr[k][c * OWN + o] = kvl[k, jnp.maximum(tab_ref[2 * o + c], 0)]

    def relay_copy(k, p, core):
        at = core * OWN + p
        return rcopy(arr[k].at[at], arr[k].at[at], b_s.at[k, p], b_r.at[k, p], (o, mate))

    def relay(k, lo, hi):
        def step(i, _):
            p = lax.rem(o - i + OWN, OWN)
            rcopy(
                snd.at[k, 1], arr[k].at[c * OWN + p], a_s.at[k, 1], a_r.at[k, p], (o, mate)
            ).wait_recv()
            relay_copy(k, p, c).start()
            return 0

        lax.fori_loop(lo, hi, step, 0)

    def relays_done(k):
        def step(p, _):
            relay_copy(k, p, 1 - c).wait_recv()
            return 0

        lax.fori_loop(0, OWN, step, 0)

    send_kind(0)
    relay_copy(0, o, c).start()
    send_kind(1)
    relay_copy(1, o, c).start()

    key_at = lax.broadcasted_iota(jnp.int32, (128, ROWS), 0)
    tok_at = lax.rem(lax.broadcasted_iota(jnp.int32, (128, ROWS), 1), 128)
    so = jnp.where(key_at <= tok_at, mm(ownx[0], qt[...]), MASKED)
    eo_ref[...] = so
    dpo_ref[...] = mm(ownx[1], dot_[...])
    top = fold(so, jnp.max)

    relay(0, 1, OWN)
    relays_done(0)

    def score(j, top):
        long = pblk[retr[o, j]] >= 2
        kj = arrk[pos[j]]
        s0 = mm(kj[:128], qt[...])
        e_ref[j, 0:128] = s0
        s1 = jnp.where(long, mm(kj[128:], qt[...]), MASKED)
        e_ref[j, 128:256] = s1
        return jnp.maximum(top, jnp.maximum(fold(s0, jnp.max), fold(s1, jnp.max)))

    top = lax.fori_loop(0, RET, score, top)
    kk = SCALE * LOG2E
    mrow = jnp.max(top, axis=0, keepdims=True) * kk

    eo = jnp.exp2(eo_ref[...] * kk - mrow)
    eo_ref[...] = eo
    tot = fold(eo, jnp.sum)

    def expo(j, tot):
        for half in range(2):
            rows = pl.ds(half * 128, 128)
            e = jnp.exp2(e_ref[j, rows] * kk - mrow)
            e_ref[j, rows] = e
            tot = tot + fold(e, jnp.sum)
        return tot

    tot = lax.fori_loop(0, RET, expo, tot)
    rl = 1.0 / jnp.sum(tot, axis=0, keepdims=True)
    for h in range(HD):
        rows = pl.ds(h * 128, 128)
        rcol = jnp.broadcast_to(rl[:, h * 128:(h + 1) * 128], (128, 128)).T
        dosn[rows, :] = (dos[rows, :].astype(F32) * rcol).astype(BF)

    def vgrad(j, _):
        dkv[1, j] = mm(e_ref[j].astype(BF), dosn[...])
        return 0

    lax.fori_loop(0, RET, vgrad, 0)
    dvo = mm(eo_ref[...].astype(BF), dosn[...])

    def give_copy(k, n):
        part = pl.ds(n * 4, 4)
        return rcopy(
            give.at[k, part], got.at[k, part], g_s.at[k, n], g_r.at[k, n], (o, mate)
        )

    def give_all(k):
        def step(n, _):
            for m in range(4):
                p = n * 4 + m
                give[k, p] = dkv[k, inv[(1 - c) * OWN + p]].astype(BF)
            give_copy(k, n).start()
            return 0

        lax.fori_loop(0, 4, step, 0)

    def home(k, p):
        return rcopy(
            sret.at[k, p], ret_ref.at[c * OWN + o], t_s.at[k, p], t_r.at[c * OWN + o],
            (p, 2 * zi + k),
        )

    def home_self(k):
        return pltpu.make_async_copy(sret.at[k, o], ret_ref.at[c * OWN + o], t_s.at[k, o])

    def return_part(k, n):
        give_copy(k, n).wait_recv()

        def step(m, _):
            p = n * 4 + m
            sret[k, p] = (dkv[k, inv[c * OWN + p]] + got[k, p].astype(F32)).astype(BF)

            @pl.when((p != o) | (c != k))
            def _():
                home(k, p).start()

            @pl.when((p == o) & (c == k))
            def _():
                home_self(k).start()

            return 0

        lax.fori_loop(0, 4, step, 0)

    give_all(1)
    relay(1, 1, 9)
    for n in range(4):
        return_part(1, n)
    relay(1, 9, OWN)
    relays_done(1)

    du = fold(eo_ref[...] * dpo_ref[...], jnp.sum)

    def pgrad(j, du):
        vj = arrv[pos[j]]
        for half in range(2):
            rows = pl.ds(half * 128, 128)
            d = mm(vj[half * 128:(half + 1) * 128], dot_[...])
            dp_ref[j, rows] = d
            du = du + fold(e_ref[j, rows] * d, jnp.sum)
        return du

    du = lax.fori_loop(0, RET, pgrad, du)
    delta = jnp.sum(du, axis=0, keepdims=True) * rl
    fa = rl * SCALE
    fb = fa * delta

    tn = (((0,), (0,)), ((), ()))
    dso = (eo_ref[...] * (dpo_ref[...] * fa - fb)).astype(BF)
    dqt[...] = lax.dot_general(ownx[0], dso, tn, preferred_element_type=F32)
    dko = mm(dso, qs[...])

    def sgrad(j, _):
        ds = (e_ref[j] * (dp_ref[j] * fa - fb)).astype(BF)
        dqt[...] += lax.dot_general(arrk[pos[j]], ds, tn, preferred_element_type=F32)
        dkv[0, j] = mm(ds, qs[...])
        return 0

    lax.fori_loop(0, RET, sgrad, 0)

    is0 = c == 0
    ogive[...] = jnp.where(is0, dvo, dko).astype(BF)
    own_give = rcopy(ogive, ogot, pre_s.at[2], pre_r.at[2], (o, mate))
    own_give.start()
    own_keep = jnp.where(is0, dko, dvo)

    load_w.wait()
    dqb = jnp.concatenate(
        [dqt[:, h * 128:(h + 1) * 128].T.astype(BF) for h in range(HD)], axis=1
    )

    def project(n, _):
        wn = wv[pl.ds(pl.multiple_of(n * CBW, CBW), CBW), :]
        part = lax.dot_general(
            dqb, wn, (((1,), (1,)), ((), ())), preferred_element_type=F32
        )
        rows = pl.ds(pl.multiple_of(n * 16, 16), 16)
        for dz in range(8):
            for core in range(2):
                block = part[(2 * dz + core) * 8:(2 * dz + core) * 8 + 8]
                both = jnp.concatenate([block[:, :512], block[:, 512:]], axis=0)
                zall[core, dz, rows, :] = both.astype(BF)
        return 0

    lax.fori_loop(0, CB, project, 0)
    zx = rcopy(zall.at[1 - c], zgot, pre_s.at[3], pre_r.at[3], (o, mate))
    zx.start()
    give_all(0)
    zx.wait_recv()

    def term(step):
        at = lax.rem(zi + step + 8, 8)
        return zall[c, at].astype(F32) + zgot[at].astype(F32)

    def chain(way, step):
        dev = (o, zup if way == 0 else zdn)
        if step == 0:
            part = pl.ds(64 * way, 64)
            return rcopy(
                zsnd.at[way, 0, part], zrcv.at[way, 0, part],
                z_s.at[way, 0], z_r.at[way, 0], dev,
            )
        return rcopy(
            zsnd.at[way, step], zrcv.at[way, step], z_s.at[way, step], z_r.at[way, step], dev
        )

    def chain_step(step):
        for way in range(2):
            sign = 1 - 2 * way
            if step == 0:
                zsnd[way, 0] = term(4).astype(BF)
            else:
                chain(way, step - 1).wait_recv()
                mine = term(sign * (4 - step))
                part = zrcv[way, step - 1]
                if step == 1:
                    lo = slice(64 * way, 64 * way + 64)
                    rest = slice(64 - 64 * way, 128 - 64 * way)
                    zsnd[way, step, lo] = (mine[lo] + part[lo].astype(F32)).astype(BF)
                    zsnd[way, step, rest] = mine[rest].astype(BF)
                else:
                    zsnd[way, step] = (mine + part.astype(F32)).astype(BF)
            chain(way, step).start()

    chain_step(0)
    return_part(0, 0)
    chain_step(1)
    return_part(0, 1)
    return_part(0, 2)
    chain_step(2)
    return_part(0, 3)
    own_give.wait_recv()
    og_ref[...] = (own_keep + ogot[...].astype(F32)).astype(BF)
    chain_step(3)
    for way in range(2):
        chain(way, 3).wait_recv()
    total = term(0) + zrcv[0, 3].astype(F32) + zrcv[1, 3].astype(F32)
    for n in range(CB):
        for m in range(2):
            gi_ref[:, n * CBW + m * 512:n * CBW + (m + 1) * 512] = total[
                n * 16 + m * 8:n * 16 + m * 8 + 8
            ].astype(BF)

    def drain(i, _):
        for k in range(2):
            hop(k, i).wait_send()
        return 0

    lax.fori_loop(1, OWN, drain, 0)

    def drain2(p, _):
        for k in range(2):
            relay_copy(k, p, c).wait_send()

            @pl.when((p != o) | (c != k))
            def _():
                home(k, p).wait_send()

            @pl.when((p == o) & (c == k))
            def _():
                home_self(k).wait()

        for r in range(2):
            @pl.when((p != o) | (c != r))
            def _():
                rcopy(
                    sret.at[0, p], ret_ref.at[r * OWN + p], t_s.at[0, p], t_r.at[r * OWN + p],
                    (o, mate),
                ).wait_recv()

        return 0

    lax.fori_loop(0, OWN, drain2, 0)
    for k in range(2):
        for n in range(4):
            give_copy(k, n).wait_send()
    own_give.wait_send()
    zx.wait_send()
    for way in range(2):
        for step in range(4):
            chain(way, step).wait_send()


def add_kernel(tab_ref, ret_ref, gi_ref, og_ref, out_ref, gi_out, og_out, acc):
    gi_out[...] = gi_ref[...]
    og_out[...] = og_ref[...]
    acc[...] = jnp.zeros_like(acc)

    def step(s, _):
        for r in range(2):
            at = tab_ref[2 * s + r]

            @pl.when(at >= 0)
            def _():
                acc[at] += ret_ref[r * OWN + s].astype(F32)

        return 0

    lax.fori_loop(0, OWN, step, 0)
    out_ref[...] = acc[...].astype(BF)


def body(queries, out_grad, own_kv, passage_kv, query_weight, retrieval, passage_slot, passage_blocks):
    vm = pl.BlockSpec(memory_space=pltpu.VMEM)
    sm = pl.BlockSpec(memory_space=pltpu.SMEM)
    hb = pl.BlockSpec(memory_space=pl.ANY)
    block = (PLEN, HS)
    dma = pltpu.SemaphoreType.DMA
    gi, og, ret, tab = pl.pallas_call(
        main_kernel,
        out_shape=(
            jax.ShapeDtypeStruct((8, 8192), BF),
            jax.ShapeDtypeStruct((128, HS), BF),
            jax.ShapeDtypeStruct((2 * OWN,) + block, BF),
            jax.ShapeDtypeStruct((2 * OWN,), jnp.int32),
        ),
        in_specs=[sm, sm, sm, vm, vm, vm, hb, hb],
        out_specs=(vm, vm, hb, sm),
        scratch_shapes=[
            pltpu.VMEM((2, OWN) + block, BF),
            pltpu.VMEM((2, 128, HS), BF),
            pltpu.VMEM((2, OWN) + block, BF),
            pltpu.VMEM((2 * OWN,) + block, BF),
            pltpu.VMEM((2 * OWN,) + block, BF),
            pltpu.VMEM((RET, PLEN, ROWS), F32),
            pltpu.VMEM((128, ROWS), F32),
            pltpu.VMEM((RET, PLEN, ROWS), F32),
            pltpu.VMEM((128, ROWS), F32),
            pltpu.VMEM((ROWS, HS), BF),
            pltpu.VMEM((HS, ROWS), BF),
            pltpu.VMEM((ROWS, HS), BF),
            pltpu.VMEM((HS, ROWS), BF),
            pltpu.VMEM((ROWS, HS), BF),
            pltpu.VMEM((2, RET) + block, F32),
            pltpu.VMEM((HS, ROWS), F32),
            pltpu.VMEM((2, OWN) + block, BF),
            pltpu.VMEM((2, OWN) + block, BF),
            pltpu.VMEM((2, OWN) + block, BF),
            pltpu.VMEM((8192, 512), BF),
            pltpu.VMEM((2, 8, 128, 512), BF),
            pltpu.VMEM((8, 128, 512), BF),
            pltpu.VMEM((2, 4, 128, 512), BF),
            pltpu.VMEM((2, 4, 128, 512), BF),
            pltpu.VMEM((128, HS), BF),
            pltpu.VMEM((128, HS), BF),
            pltpu.SMEM((RET,), jnp.int32),
            pltpu.SMEM((2 * OWN,), jnp.int32),
            dma((4,)), dma((4,)),
            dma((2, OWN)), dma((2, OWN)),
            dma((2, OWN)), dma((2, OWN)),
            dma((2, 4)), dma((2, 4)),
            dma((2, OWN)), dma((2 * OWN,)),
            dma((2, 4)), dma((2, 4)),
            dma((2,)),
        ],
        compiler_params=pltpu.CompilerParams(
            collective_id=0, has_side_effects=True, vmem_limit_bytes=60 * 1024 * 1024
        ),
        cost_estimate=pl.CostEstimate(flops=4_000_000_000, bytes_accessed=12_000_000, transcendentals=2_000_000),
        name="exchange_attend",
    )(
        retrieval, passage_slot, passage_blocks, queries, out_grad,
        own_kv.reshape(128, HS), passage_kv.reshape((OWN,) + block), query_weight,
    )
    pg, gi, og = pl.pallas_call(
        add_kernel,
        out_shape=(
            jax.ShapeDtypeStruct((OWN,) + block, BF),
            jax.ShapeDtypeStruct((8, 8192), BF),
            jax.ShapeDtypeStruct((128, HS), BF),
        ),
        in_specs=[sm, vm, vm, vm],
        out_specs=(vm, vm, vm),
        scratch_shapes=[pltpu.VMEM((OWN,) + block, F32)],
        compiler_params=pltpu.CompilerParams(vmem_limit_bytes=16 * 1024 * 1024),
        name="add_returns",
    )(tab, ret, gi, og)
    return gi, pg.reshape((OWN, 1) + block), og.reshape(128, 1, HS)


def solution(mesh):
    placed = (
        P("owner", "tp"),
        P("owner", "tp"),
        P("owner", "tp", None),
        P("owner", "tp", None, None),
        P(None, "tp"),
        P(),
        P(),
        P(),
    )
    return jax.shard_map(
        body,
        mesh=mesh,
        in_specs=placed,
        out_specs=(P(("owner", "tp"), None), P("owner", "tp", None, None), P("owner", "tp", None)),
        check_vma=False,
    )
```

```python
import functools
import math

import jax
import jax.numpy as jnp
from jax import lax
from jax.experimental import pallas as pl
from jax.experimental.pallas import tpu as pltpu
from jax.sharding import PartitionSpec as P

MESH = pl.DeviceIdType.MESH
BF = jnp.bfloat16
F32 = jnp.float32
MASKED = -1e30
OWN = 16
RET = 16
PLEN = 256
HS = 128
HD = 4
ROWS = 512
SCALE = HS ** -0.5
LOG2E = 1.0 / math.log(2.0)
CB = 8
CBW = 1024


def mm(a, b):
    return lax.dot_general(a, b, (((1,), (0,)), ((), ())), preferred_element_type=F32)


def fold(x, op):
    return op(x.reshape(x.shape[0] // 8, 8, x.shape[1]), axis=0)


def main_kernel(
    retr_in, pslot_in, pblk_in, q_in, do_in, own_in, pkv_ref, w_ref,
    gi_ref, og_ref, ret_ref, tab_ref,
    retr, pslot, pblk, q_ref, do_ref,
    kloc, vloc, ownx, snd, arrk, arrv, e_ref, eo_ref, dp_ref, dpo_ref, ds_ref, qs, qt, dos, dot_,
    dosn, dkv, dqt, give, got, sret, wv, zall, zgot, zsnd, zrcv, ogive, ogot,
    pos, inv, pre_s, pre_r, a_s, a_r, b_s, b_r, g_s, g_r, t_s, t_r, z_s, z_r, misc,
):
    o = lax.axis_index("owner")
    t = lax.axis_index("tp")
    c = lax.rem(t, 2)
    zi = t // 2
    mate = t + 1 - 2 * c
    arr = (arrk, arrv)
    loc = (kloc, vloc)

    def rcopy(src, dst, ss, rs, dev):
        return pltpu.make_async_remote_copy(
            src_ref=src, dst_ref=dst, send_sem=ss, recv_sem=rs, device_id=dev, device_id_type=MESH
        )

    def load_kv(k):
        return pltpu.make_async_copy(pkv_ref, loc[k], misc.at[0])

    load_w = pltpu.make_async_copy(w_ref, wv, misc.at[1])
    small = [
        pltpu.make_async_copy(src, dst, misc.at[2 + n])
        for n, (src, dst) in enumerate(
            ((pslot_in, pslot), (retr_in, retr), (pblk_in, pblk),
             (own_in, ownx.at[c]), (q_in, q_ref), (do_in, do_ref))
        )
    ]
    for copy in small[:2]:
        copy.start()
    for k in range(2):
        pl.when(c == k)(load_kv(k).start)

    def shift(n):
        m = jnp.where(n >= 15, 10, n + (n >= 10).astype(jnp.int32))
        return lax.rem(m + 2, 4), lax.rem(m // 4 + 2, 4)

    def peer(n):
        dx, dy = shift(n)
        return lax.rem(o // 4 + dy, 4) * 4 + lax.rem(lax.rem(o, 4) + dx, 4)

    def origin(n):
        dx, dy = shift(n)
        return lax.rem(o // 4 - dy + 4, 4) * 4 + lax.rem(lax.rem(o, 4) - dx + 4, 4)

    bar = pltpu.get_barrier_semaphore()

    def greet(n, _):
        s = peer(n)
        pl.semaphore_signal(bar, inc=1, device_id=(s, t), device_id_type=MESH)
        pl.semaphore_signal(bar, inc=1, device_id=(s, mate), device_id_type=MESH)
        return 0

    lax.fori_loop(0, 15, greet, 0)
    zup = lax.rem(zi + 1, 8) * 2 + c
    zdn = lax.rem(zi + 7, 8) * 2 + c
    for dev in (mate, zup, zdn):
        pl.semaphore_signal(bar, inc=1, device_id=(o, dev), device_id_type=MESH)
    for copy in small[2:]:
        copy.start()
    load_w.start()
    for copy in small[:2]:
        copy.wait()

    def table(s, _):
        first = jnp.int32(-1)
        second = jnp.int32(-1)
        for j in range(RET):
            slot = pslot[retr[s, j]]
            hit = (slot >> 4) == o
            local = slot & 15
            second = jnp.where(hit & (first >= 0), local, second)
            first = jnp.where(hit & (first < 0), local, first)
        tab_ref[2 * s] = first
        tab_ref[2 * s + 1] = second
        return 0

    lax.fori_loop(0, OWN, table, 0)
    small[3].wait()
    pl.semaphore_wait(bar, 33)

    own_x = rcopy(ownx.at[c], ownx.at[c], pre_s.at[1], pre_r.at[1], (o, mate))

    def swap_kv(k):
        return rcopy(loc[k], loc[k], pre_s.at[0], pre_r.at[0], (o, mate))

    def hop(k, n):
        return rcopy(
            snd.at[k, n], arr[k].at[c * OWN + o], a_s.at[k, n], a_r.at[k, o], (peer(n), t)
        )

    def send(k, lo, hi):
        def step(n, _):
            at = jnp.maximum(tab_ref[2 * peer(n) + c], 0)
            snd[k, n] = loc[k][at]
            hop(k, n).start()
            return 0

        lax.fori_loop(lo, hi, step, 0)

    def relay_copy(k, p, core):
        at = core * OWN + p
        return rcopy(arr[k].at[at], arr[k].at[at], b_s.at[k, p], b_r.at[k, p], (o, mate))

    def keep_own(k):
        arr[k][c * OWN + o] = loc[k][jnp.maximum(tab_ref[2 * o + c], 0)]
        relay_copy(k, o, c).start()

    @pl.when(c == 0)
    def _():
        load_kv(0).wait()
        swap_kv(0).start()
        own_x.start()
        send(0, 0, 15)
        keep_own(0)
        swap_kv(1).wait_recv()
        keep_own(1)

    @pl.when(c == 1)
    def _():
        load_kv(1).wait()
        swap_kv(1).start()
        own_x.start()
        send(1, 0, 3)
        swap_kv(0).wait_recv()
        send(0, 0, 15)
        keep_own(0)
        keep_own(1)

    owners = []
    for j in range(RET):
        ow = pslot[retr[o, j]] >> 4
        rank = jnp.int32(0)
        for prev in owners:
            rank = rank + (prev == ow).astype(jnp.int32)
        owners.append(ow)
        pos[j] = jnp.minimum(rank, 1) * OWN + ow

    def inverse(n, _):
        at = jnp.int32(0)
        for j in range(RET):
            at = jnp.where(pos[j] == n, j, at)
        inv[n] = at
        return 0

    lax.fori_loop(0, 2 * OWN, inverse, 0)

    for copy in small[4:]:
        copy.wait()
    for h in range(HD):
        rows = pl.ds(h * 128, 128)
        qh = q_ref[:, h * 128:(h + 1) * 128]
        dh = do_ref[:, h * 128:(h + 1) * 128]
        qs[rows, :] = qh
        dos[rows, :] = dh
        qt[:, rows] = qh.T
        dot_[:, rows] = dh.T
    own_x.wait()
    small[2].wait()

    def relay(k, lo, hi):
        def step(n, _):
            p = origin(n)
            rcopy(
                snd.at[k, 1], arr[k].at[c * OWN + p], a_s.at[k, 1], a_r.at[k, p], (o, mate)
            ).wait_recv()
            relay_copy(k, p, c).start()
            return 0

        lax.fori_loop(lo, hi, step, 0)

    def relays_done(k):
        def step(p, _):
            relay_copy(k, p, 1 - c).wait_recv()
            return 0

        lax.fori_loop(0, OWN, step, 0)

    key_at = lax.broadcasted_iota(jnp.int32, (128, ROWS), 0)
    tok_at = lax.rem(lax.broadcasted_iota(jnp.int32, (128, ROWS), 1), 128)
    so = jnp.where(key_at <= tok_at, mm(ownx[0], qt[...]), MASKED)
    eo_ref[...] = so
    dpo_ref[...] = mm(ownx[1], dot_[...])
    top = fold(so, jnp.max)

    relay(0, 0, 7)
    pl.when(c == 0)(lambda: send(1, 0, 3))
    for n in range(8):
        relay(0, 7 + n, 8 + n)
        send(1, 3 + 12 * n // 8, 3 + 12 * (n + 1) // 8)
    relays_done(0)

    def score(j, top):
        long = pblk[retr[o, j]] >= 2
        kj = arrk[pos[j]]
        s0 = mm(kj[:128], qt[...])
        e_ref[j, 0:128] = s0
        s1 = jnp.where(long, mm(kj[128:], qt[...]), MASKED)
        e_ref[j, 128:256] = s1
        return jnp.maximum(top, jnp.maximum(fold(s0, jnp.max), fold(s1, jnp.max)))

    top = lax.fori_loop(0, RET, score, top)
    kk = SCALE * LOG2E
    mrow = jnp.max(top, axis=0, keepdims=True) * kk

    eo = jnp.exp2(eo_ref[...] * kk - mrow)
    eo_ref[...] = eo
    tot = fold(eo, jnp.sum)

    def expo(j, tot):
        for half in range(2):
            rows = pl.ds(half * 128, 128)
            e = jnp.exp2(e_ref[j, rows] * kk - mrow)
            e_ref[j, rows] = e
            tot = tot + fold(e, jnp.sum)
        return tot

    tot = lax.fori_loop(0, RET, expo, tot)
    rl = 1.0 / jnp.sum(tot, axis=0, keepdims=True)
    for h in range(HD):
        rows = pl.ds(h * 128, 128)
        rcol = jnp.broadcast_to(rl[:, h * 128:(h + 1) * 128], (128, 128)).T
        dosn[rows, :] = (dos[rows, :].astype(F32) * rcol).astype(BF)

    def vgrad(j, _):
        dkv[j] = mm(e_ref[j].astype(BF), dosn[...])
        return 0

    relay(1, 0, 3)
    lax.fori_loop(0, RET // 2, vgrad, 0)
    relay(1, 3, 6)
    lax.fori_loop(RET // 2, RET, vgrad, 0)
    dvo = mm(eo_ref[...].astype(BF), dosn[...])

    def give_copy(k, n):
        part = pl.ds(n * 4, 4)
        return rcopy(
            give.at[k, part], got.at[k, part], g_s.at[k, n], g_r.at[k, n], (o, mate)
        )

    def grads(k, j):
        return dkv[j] if k else mm(ds_ref[j], qs[...])

    def give_all(k):
        def step(n, _):
            for m in range(4):
                i = n * 4 + m
                p = peer(i)
                give[k, i] = grads(k, inv[(1 - c) * OWN + p]).astype(BF)
            give_copy(k, n).start()
            return 0

        lax.fori_loop(0, 4, step, 0)

    def home(k, i):
        return rcopy(
            sret.at[k, i], ret_ref.at[c * OWN + o], t_s.at[k, i], t_r.at[c * OWN + o],
            (peer(i), 2 * zi + k),
        )

    def home_self(k):
        return pltpu.make_async_copy(sret.at[k, 15], ret_ref.at[c * OWN + o], t_s.at[k, 15])

    def return_part(k, n):
        give_copy(k, n).wait_recv()

        def step(m, _):
            i = n * 4 + m
            p = peer(i)
            sret[k, i] = (grads(k, inv[c * OWN + p]) + got[k, i].astype(F32)).astype(BF)

            @pl.when((i != 15) | (c != k))
            def _():
                home(k, i).start()

            @pl.when((i == 15) & (c == k))
            def _():
                home_self(k).start()

            return 0

        lax.fori_loop(0, 4, step, 0)

    give_all(1)
    relay(1, 6, 9)
    for n in range(4):
        return_part(1, n)
    relay(1, 9, 15)
    relays_done(1)

    du = fold(eo_ref[...] * dpo_ref[...], jnp.sum)

    def pgrad(j, du):
        vj = arrv[pos[j]]
        for half in range(2):
            rows = pl.ds(half * 128, 128)
            d = mm(vj[half * 128:(half + 1) * 128], dot_[...])
            dp_ref[j, rows] = d
            du = du + fold(e_ref[j, rows] * d, jnp.sum)
        return du

    du = lax.fori_loop(0, RET, pgrad, du)
    delta = jnp.sum(du, axis=0, keepdims=True) * rl
    fa = rl * SCALE
    fb = fa * delta

    tn = (((0,), (0,)), ((), ()))
    dso = (eo_ref[...] * (dpo_ref[...] * fa - fb)).astype(BF)
    dqt[...] = lax.dot_general(ownx[0], dso, tn, preferred_element_type=F32)
    dko = mm(dso, qs[...])

    def sgrad(j, _):
        ds = (e_ref[j] * (dp_ref[j] * fa - fb)).astype(BF)
        ds_ref[j] = ds
        dqt[...] += lax.dot_general(arrk[pos[j]], ds, tn, preferred_element_type=F32)
        return 0

    lax.fori_loop(0, RET, sgrad, 0)

    load_w.wait()
    dqb = jnp.concatenate(
        [dqt[:, h * 128:(h + 1) * 128].T.astype(BF) for h in range(HD)], axis=1
    )

    def project(n, _):
        wn = wv[pl.ds(pl.multiple_of(n * CBW, CBW), CBW), :]
        part = lax.dot_general(
            dqb, wn, (((1,), (1,)), ((), ())), preferred_element_type=F32
        )
        rows = pl.ds(pl.multiple_of(n * 16, 16), 16)
        for dz in range(8):
            for core in range(2):
                block = part[(2 * dz + core) * 8:(2 * dz + core) * 8 + 8]
                both = jnp.concatenate([block[:, :512], block[:, 512:]], axis=0)
                zall[core, dz, rows, :] = both.astype(BF)
        return 0

    def swap_z(h):
        rows = pl.ds(64 * h, 64)
        return rcopy(
            zall.at[1 - c, :, rows], zgot.at[:, rows], pre_s.at[3 + h], pre_r.at[3 + h], (o, mate)
        )

    for h in range(2):
        lax.fori_loop(h * 4, h * 4 + 4, project, 0)
        swap_z(h).start()

    is0 = c == 0
    ogive[...] = jnp.where(is0, dvo, dko).astype(BF)
    own_give = rcopy(ogive, ogot, pre_s.at[2], pre_r.at[2], (o, mate))
    own_give.start()
    own_keep = jnp.where(is0, dko, dvo)

    give_all(0)

    def term(dist, h):
        at = lax.rem(zi + dist + 8, 8)
        rows = pl.ds(64 * h, 64)
        return zall[c, at, rows].astype(F32) + zgot[at, rows].astype(F32)

    def chain(way, step, h):
        rows = pl.ds(64 * h, 64)
        return rcopy(
            zsnd.at[way, step, rows], zrcv.at[way, step, rows],
            z_s.at[way, 2 * step + h], z_r.at[way, 2 * step + h],
            (o, zup if way == 0 else zdn),
        )

    def chain_step(step, same):
        for way in range(2):
            h = way if same else 1 - way
            rows = pl.ds(64 * h, 64)
            mine = term((1 - 2 * way) * (4 - step), h)
            if step > (0 if same else 1):
                chain(way, step - 1, h).wait_recv()
                mine = mine + zrcv[way, step - 1, rows].astype(F32)
            zsnd[way, step, rows] = mine.astype(BF)
            chain(way, step, h).start()

    for h in range(2):
        swap_z(h).wait_recv()
    chain_step(0, True)
    chain_step(1, False)
    return_part(0, 0)
    chain_step(1, True)
    return_part(0, 1)
    chain_step(2, False)
    return_part(0, 2)
    chain_step(2, True)
    return_part(0, 3)
    chain_step(3, False)
    own_give.wait_recv()
    og_ref[...] = (own_keep + ogot[...].astype(F32)).astype(BF)
    chain_step(3, True)
    for h in range(2):
        total = term(0, h)
        for way in (1 - h, h):
            chain(way, 3, h).wait_recv()
            total = total + zrcv[way, 3, pl.ds(64 * h, 64)].astype(F32)
        for n in range(4):
            for m in range(2):
                at = (h * 4 + n) * CBW + m * 512
                gi_ref[:, at:at + 512] = total[n * 16 + m * 8:n * 16 + m * 8 + 8].astype(BF)

    for k in range(2):
        pl.when(c == k)(swap_kv(k).wait_send)

    def drain(n, _):
        for k in range(2):
            hop(k, n).wait_send()
        return 0

    lax.fori_loop(0, 15, drain, 0)

    def drain2(p, _):
        for k in range(2):
            relay_copy(k, p, c).wait_send()

            @pl.when((p != 15) | (c != k))
            def _():
                home(k, p).wait_send()

            @pl.when((p == 15) & (c == k))
            def _():
                home_self(k).wait()

        for r in range(2):
            @pl.when((p != o) | (c != r))
            def _():
                rcopy(
                    sret.at[0, p], ret_ref.at[r * OWN + p], t_s.at[0, p], t_r.at[r * OWN + p],
                    (o, mate),
                ).wait_recv()

        return 0

    lax.fori_loop(0, OWN, drain2, 0)
    for k in range(2):
        for n in range(4):
            give_copy(k, n).wait_send()
    own_give.wait_send()
    for h in range(2):
        swap_z(h).wait_send()
    for way in range(2):
        for step in range(4):
            for h in range(2):
                if step > 0 or h == way:
                    chain(way, step, h).wait_send()


def add_kernel(
    tab_in, ret_in, gi_in, og_in, out_ref, gi_out, og_out, tab, ret, acc, outv, giv, ogv, sems
):
    get_tab = pltpu.make_async_copy(tab_in, tab, sems.at[0])
    get_tab.start()
    parts = [
        pltpu.make_async_copy(ret_in.at[pl.ds(8 * n, 8)], ret.at[pl.ds(8 * n, 8)], sems.at[1 + n])
        for n in range(4)
    ]
    for copy in parts:
        copy.start()
    fetch = [
        pltpu.make_async_copy(gi_in, giv, sems.at[5]),
        pltpu.make_async_copy(og_in, ogv, sems.at[6]),
    ]
    for copy in fetch:
        copy.start()
    acc[...] = jnp.zeros_like(acc)
    get_tab.wait()
    for copy in fetch:
        copy.wait()
    rest = [
        pltpu.make_async_copy(giv, gi_out, sems.at[5]),
        pltpu.make_async_copy(ogv, og_out, sems.at[6]),
    ]
    for copy in rest:
        copy.start()
    for n in range(4):
        parts[n].wait()

        def step(m, _):
            i = n * 8 + m
            at = tab[2 * lax.rem(i, OWN) + i // OWN]

            @pl.when(at >= 0)
            def _():
                acc[at] += ret[i].astype(F32)

            return 0

        lax.fori_loop(0, 8, step, 0)
    done = []
    for n in range(4):
        part = pl.ds(4 * n, 4)
        outv[part] = acc[part].astype(BF)
        done.append(pltpu.make_async_copy(outv.at[part], out_ref.at[part], sems.at[7 + n]))
        done[-1].start()
    for copy in rest + done:
        copy.wait()


def body(queries, out_grad, own_kv, passage_kv, query_weight, retrieval, passage_slot, passage_blocks):
    vm = pl.BlockSpec(memory_space=pltpu.VMEM)
    sm = pl.BlockSpec(memory_space=pltpu.SMEM)
    hb = pl.BlockSpec(memory_space=pltpu.HBM)
    block = (PLEN, HS)
    dma = pltpu.SemaphoreType.DMA
    gi, og, ret, tab = pl.pallas_call(
        main_kernel,
        out_shape=(
            jax.ShapeDtypeStruct((8, 8192), BF),
            jax.ShapeDtypeStruct((128, HS), BF),
            jax.ShapeDtypeStruct((2 * OWN,) + block, BF),
            jax.ShapeDtypeStruct((2 * OWN,), jnp.int32),
        ),
        in_specs=[hb] * 8,
        out_specs=(vm, vm, hb, sm),
        scratch_shapes=[
            pltpu.SMEM((RET, OWN), jnp.int32),
            pltpu.SMEM((RET * OWN,), jnp.int32),
            pltpu.SMEM((RET * OWN,), jnp.int32),
            pltpu.VMEM((128, ROWS), BF),
            pltpu.VMEM((128, ROWS), BF),
            pltpu.VMEM((OWN,) + block, BF),
            pltpu.VMEM((OWN,) + block, BF),
            pltpu.VMEM((2, 128, HS), BF),
            pltpu.VMEM((2, OWN) + block, BF),
            pltpu.VMEM((2 * OWN,) + block, BF),
            pltpu.VMEM((2 * OWN,) + block, BF),
            pltpu.VMEM((RET, PLEN, ROWS), F32),
            pltpu.VMEM((128, ROWS), F32),
            pltpu.VMEM((RET, PLEN, ROWS), F32),
            pltpu.VMEM((128, ROWS), F32),
            pltpu.VMEM((RET, PLEN, ROWS), BF),
            pltpu.VMEM((ROWS, HS), BF),
            pltpu.VMEM((HS, ROWS), BF),
            pltpu.VMEM((ROWS, HS), BF),
            pltpu.VMEM((HS, ROWS), BF),
            pltpu.VMEM((ROWS, HS), BF),
            pltpu.VMEM((RET,) + block, F32),
            pltpu.VMEM((HS, ROWS), F32),
            pltpu.VMEM((2, OWN) + block, BF),
            pltpu.VMEM((2, OWN) + block, BF),
            pltpu.VMEM((2, OWN) + block, BF),
            pltpu.VMEM((8192, 512), BF),
            pltpu.VMEM((2, 8, 128, 512), BF),
            pltpu.VMEM((8, 128, 512), BF),
            pltpu.VMEM((2, 4, 128, 512), BF),
            pltpu.VMEM((2, 4, 128, 512), BF),
            pltpu.VMEM((128, HS), BF),
            pltpu.VMEM((128, HS), BF),
            pltpu.SMEM((RET,), jnp.int32),
            pltpu.SMEM((2 * OWN,), jnp.int32),
            dma((5,)), dma((5,)),
            dma((2, OWN)), dma((2, OWN)),
            dma((2, OWN)), dma((2, OWN)),
            dma((2, 4)), dma((2, 4)),
            dma((2, OWN)), dma((2 * OWN,)),
            dma((2, 8)), dma((2, 8)),
            dma((8,)),
        ],
        compiler_params=pltpu.CompilerParams(
            collective_id=0, has_side_effects=True, vmem_limit_bytes=60 * 1024 * 1024
        ),
        cost_estimate=pl.CostEstimate(flops=4_000_000_000, bytes_accessed=12_000_000, transcendentals=2_000_000),
        name="exchange_attend",
    )(
        retrieval, passage_slot, passage_blocks, queries, out_grad,
        own_kv.reshape(128, HS), passage_kv.reshape((OWN,) + block), query_weight,
    )
    pg, gi, og = pl.pallas_call(
        add_kernel,
        out_shape=(
            jax.ShapeDtypeStruct((OWN,) + block, BF),
            jax.ShapeDtypeStruct((8, 8192), BF),
            jax.ShapeDtypeStruct((128, HS), BF),
        ),
        in_specs=[hb] * 4,
        out_specs=(hb, hb, hb),
        scratch_shapes=[
            pltpu.SMEM((2 * OWN,), jnp.int32),
            pltpu.VMEM((2 * OWN,) + block, BF),
            pltpu.VMEM((OWN,) + block, F32),
            pltpu.VMEM((OWN,) + block, BF),
            pltpu.VMEM((8, 8192), BF),
            pltpu.VMEM((128, HS), BF),
            dma((11,)),
        ],
        compiler_params=pltpu.CompilerParams(vmem_limit_bytes=60 * 1024 * 1024),
        name="add_returns",
    )(tab, ret, gi, og)
    return gi, pg.reshape((OWN, 1) + block), og.reshape(128, 1, HS)


def solution(mesh):
    placed = (
        P("owner", "tp"),
        P("owner", "tp"),
        P("owner", "tp", None),
        P("owner", "tp", None, None),
        P(None, "tp"),
        P(),
        P(),
        P(),
    )
    return jax.shard_map(
        body,
        mesh=mesh,
        in_specs=placed,
        out_specs=(P(("owner", "tp"), None), P("owner", "tp", None, None), P("owner", "tp", None)),
        check_vma=False,
    )
```

```python
import functools
import math

import jax
import jax.numpy as jnp
from jax import lax
from jax.experimental import pallas as pl
from jax.experimental.pallas import tpu as pltpu
from jax.sharding import PartitionSpec as P

MESH = pl.DeviceIdType.MESH
BF = jnp.bfloat16
F32 = jnp.float32
MASKED = -1e30
OWN = 16
RET = 16
PLEN = 256
HS = 128
HD = 4
ROWS = 512
SCALE = HS ** -0.5
LOG2E = 1.0 / math.log(2.0)
CB = 8
CBW = 1024


def mm(a, b):
    return lax.dot_general(a, b, (((1,), (0,)), ((), ())), preferred_element_type=F32)


def fold(x, op):
    return op(x.reshape(x.shape[0] // 8, 8, x.shape[1]), axis=0)


def main_kernel(
    retr_in, pslot_in, pblk_in, q_in, do_in, own_in, pkv_ref, w_ref,
    gi_ref, og_ref, ret_ref, tab_ref,
    retr, pslot, pblk, q_ref, do_ref,
    kloc, vloc, ownx, snd, arrk, arrv, e_ref, eo_ref, dp_ref, dpo_ref, ds_ref, qs, qt, dos, dot_,
    dosn, dkv, dqt, give, got, sret, wv, zall, zgot, zsnd, zrcv, ogive, ogot,
    pos, inv, pre_s, pre_r, a_s, a_r, b_s, b_r, g_s, g_r, t_s, t_r, z_s, z_r, misc,
):
    o = lax.axis_index("owner")
    t = lax.axis_index("tp")
    c = lax.rem(t, 2)
    zi = t // 2
    mate = t + 1 - 2 * c
    arr = (arrk, arrv)
    loc = (kloc, vloc)

    def rcopy(src, dst, ss, rs, dev):
        return pltpu.make_async_remote_copy(
            src_ref=src, dst_ref=dst, send_sem=ss, recv_sem=rs, device_id=dev, device_id_type=MESH
        )

    def load_kv(k):
        return pltpu.make_async_copy(pkv_ref, loc[k], misc.at[0])

    load_w = pltpu.make_async_copy(w_ref, wv, misc.at[1])
    small = [
        pltpu.make_async_copy(src, dst, misc.at[2 + n])
        for n, (src, dst) in enumerate(
            ((pslot_in, pslot), (retr_in, retr), (pblk_in, pblk),
             (own_in, ownx.at[c]), (q_in, q_ref), (do_in, do_ref))
        )
    ]
    for copy in small[:2]:
        copy.start()
    for k in range(2):
        pl.when(c == k)(load_kv(k).start)

    def shift(n):
        m = jnp.where(n >= 15, 10, n + (n >= 10).astype(jnp.int32))
        return lax.rem(m + 2, 4), lax.rem(m // 4 + 2, 4)

    def peer(n):
        dx, dy = shift(n)
        return lax.rem(o // 4 + dy, 4) * 4 + lax.rem(lax.rem(o, 4) + dx, 4)

    def origin(n):
        dx, dy = shift(n)
        return lax.rem(o // 4 - dy + 4, 4) * 4 + lax.rem(lax.rem(o, 4) - dx + 4, 4)

    bar = pltpu.get_barrier_semaphore()

    def greet(n, _):
        s = peer(n)
        pl.semaphore_signal(bar, inc=1, device_id=(s, t), device_id_type=MESH)
        pl.semaphore_signal(bar, inc=1, device_id=(s, mate), device_id_type=MESH)
        return 0

    lax.fori_loop(0, 15, greet, 0)
    zup = lax.rem(zi + 1, 8) * 2 + c
    zdn = lax.rem(zi + 7, 8) * 2 + c
    for dev in (mate, zup, zdn):
        pl.semaphore_signal(bar, inc=1, device_id=(o, dev), device_id_type=MESH)
    for copy in small[2:]:
        copy.start()
    load_w.start()
    for copy in small[:2]:
        copy.wait()

    def table(s, _):
        first = jnp.int32(-1)
        second = jnp.int32(-1)
        for j in range(RET):
            slot = pslot[retr[s, j]]
            hit = (slot >> 4) == o
            local = slot & 15
            second = jnp.where(hit & (first >= 0), local, second)
            first = jnp.where(hit & (first < 0), local, first)
        tab_ref[2 * s] = first
        tab_ref[2 * s + 1] = second
        return 0

    lax.fori_loop(0, OWN, table, 0)
    small[3].wait()
    pl.semaphore_wait(bar, 33)

    own_x = rcopy(ownx.at[c], ownx.at[c], pre_s.at[1], pre_r.at[1], (o, mate))

    def swap_kv(k):
        return rcopy(loc[k], loc[k], pre_s.at[0], pre_r.at[0], (o, mate))

    def hop(k, n):
        return rcopy(
            snd.at[k, n], arr[k].at[c * OWN + o], a_s.at[k, n], a_r.at[k, o], (peer(n), t)
        )

    def send(k, lo, hi):
        def step(n, _):
            at = jnp.maximum(tab_ref[2 * peer(n) + c], 0)
            snd[k, n] = loc[k][at]
            hop(k, n).start()
            return 0

        lax.fori_loop(lo, hi, step, 0)

    def relay_copy(k, p, core):
        at = core * OWN + p
        return rcopy(arr[k].at[at], arr[k].at[at], b_s.at[k, p], b_r.at[k, p], (o, mate))

    def keep_own(k):
        arr[k][c * OWN + o] = loc[k][jnp.maximum(tab_ref[2 * o + c], 0)]
        relay_copy(k, o, c).start()

    @pl.when(c == 0)
    def _():
        load_kv(0).wait()
        swap_kv(0).start()
        own_x.start()
        send(0, 0, 15)
        keep_own(0)
        swap_kv(1).wait_recv()
        keep_own(1)

    @pl.when(c == 1)
    def _():
        load_kv(1).wait()
        swap_kv(1).start()
        own_x.start()
        send(1, 0, 3)
        swap_kv(0).wait_recv()
        send(0, 0, 15)
        keep_own(0)
        keep_own(1)

    owners = []
    for j in range(RET):
        ow = pslot[retr[o, j]] >> 4
        rank = jnp.int32(0)
        for prev in owners:
            rank = rank + (prev == ow).astype(jnp.int32)
        owners.append(ow)
        pos[j] = jnp.minimum(rank, 1) * OWN + ow

    def inverse(n, _):
        at = jnp.int32(0)
        for j in range(RET):
            at = jnp.where(pos[j] == n, j, at)
        inv[n] = at
        return 0

    lax.fori_loop(0, 2 * OWN, inverse, 0)

    for copy in small[4:]:
        copy.wait()
    for h in range(HD):
        rows = pl.ds(h * 128, 128)
        qh = q_ref[:, h * 128:(h + 1) * 128]
        dh = do_ref[:, h * 128:(h + 1) * 128]
        qs[rows, :] = qh
        dos[rows, :] = dh
        qt[:, rows] = qh.T
        dot_[:, rows] = dh.T
    own_x.wait()
    small[2].wait()

    def relay(k, lo, hi):
        def step(n, _):
            p = origin(n)
            rcopy(
                snd.at[k, 1], arr[k].at[c * OWN + p], a_s.at[k, 1], a_r.at[k, p], (o, mate)
            ).wait_recv()
            relay_copy(k, p, c).start()
            return 0

        lax.fori_loop(lo, hi, step, 0)

    def relays_done(k):
        def step(p, _):
            relay_copy(k, p, 1 - c).wait_recv()
            return 0

        lax.fori_loop(0, OWN, step, 0)

    key_at = lax.broadcasted_iota(jnp.int32, (128, ROWS), 0)
    tok_at = lax.rem(lax.broadcasted_iota(jnp.int32, (128, ROWS), 1), 128)
    so = jnp.where(key_at <= tok_at, mm(ownx[0], qt[...]), MASKED)
    eo_ref[...] = so
    dpo_ref[...] = mm(ownx[1], dot_[...])
    top = fold(so, jnp.max)

    relay(0, 0, 3)
    pl.when(c == 0)(lambda: send(1, 0, 3))
    for n in range(6):
        relay(0, 3 + 2 * n, 5 + 2 * n)
        send(1, 3 + 2 * n, 5 + 2 * n)
    relays_done(0)

    def score(j, top):
        long = pblk[retr[o, j]] >= 2
        kj = arrk[pos[j]]
        s0 = mm(kj[:128], qt[...])
        e_ref[j, 0:128] = s0
        s1 = jnp.where(long, mm(kj[128:], qt[...]), MASKED)
        e_ref[j, 128:256] = s1
        return jnp.maximum(top, jnp.maximum(fold(s0, jnp.max), fold(s1, jnp.max)))

    top = lax.fori_loop(0, RET, score, top, unroll=4)
    kk = SCALE * LOG2E
    mrow = jnp.max(top, axis=0, keepdims=True) * kk

    eo = jnp.exp2(eo_ref[...] * kk - mrow)
    eo_ref[...] = eo
    tot = fold(eo, jnp.sum)

    def expo(j, tot):
        for half in range(2):
            rows = pl.ds(half * 128, 128)
            e = jnp.exp2(e_ref[j, rows] * kk - mrow)
            e_ref[j, rows] = e
            tot = tot + fold(e, jnp.sum)
        return tot

    tot = lax.fori_loop(0, RET, expo, tot, unroll=4)
    rl = 1.0 / jnp.sum(tot, axis=0, keepdims=True)
    for h in range(HD):
        rows = pl.ds(h * 128, 128)
        rcol = jnp.broadcast_to(rl[:, h * 128:(h + 1) * 128], (128, 128)).T
        dosn[rows, :] = (dos[rows, :].astype(F32) * rcol).astype(BF)

    def vgrad(j, _):
        dkv[j] = mm(e_ref[j].astype(BF), dosn[...])
        return 0

    relay(1, 0, 3)
    lax.fori_loop(0, RET // 2, vgrad, 0, unroll=4)
    relay(1, 3, 6)
    lax.fori_loop(RET // 2, RET, vgrad, 0, unroll=4)
    dvo = mm(eo_ref[...].astype(BF), dosn[...])

    def give_copy(k, n):
        part = pl.ds(n * 4, 4)
        return rcopy(
            give.at[k, part], got.at[k, part], g_s.at[k, n], g_r.at[k, n], (o, mate)
        )

    def grads(k, j):
        return dkv[j] if k else mm(ds_ref[j], qs[...])

    def give_all(k):
        def step(n, _):
            for m in range(4):
                i = n * 4 + m
                p = peer(i)
                give[k, i] = grads(k, inv[(1 - c) * OWN + p]).astype(BF)
            give_copy(k, n).start()
            return 0

        lax.fori_loop(0, 4, step, 0)

    def home(k, i):
        return rcopy(
            sret.at[k, i], ret_ref.at[c * OWN + o], t_s.at[k, i], t_r.at[c * OWN + o],
            (peer(i), 2 * zi + k),
        )

    def home_self(k):
        return pltpu.make_async_copy(sret.at[k, 15], ret_ref.at[c * OWN + o], t_s.at[k, 15])

    def return_part(k, n):
        give_copy(k, n).wait_recv()

        def step(m, _):
            i = n * 4 + m
            p = peer(i)
            sret[k, i] = (grads(k, inv[c * OWN + p]) + got[k, i].astype(F32)).astype(BF)

            @pl.when((i != 15) | (c != k))
            def _():
                home(k, i).start()

            @pl.when((i == 15) & (c == k))
            def _():
                home_self(k).start()

            return 0

        lax.fori_loop(0, 4, step, 0, unroll=2)

    give_all(1)
    relay(1, 6, 9)
    for n in range(4):
        return_part(1, n)
    relay(1, 9, 15)
    relays_done(1)

    du = fold(eo_ref[...] * dpo_ref[...], jnp.sum)

    def pgrad(j, du):
        vj = arrv[pos[j]]
        for half in range(2):
            rows = pl.ds(half * 128, 128)
            d = mm(vj[half * 128:(half + 1) * 128], dot_[...])
            dp_ref[j, rows] = d
            du = du + fold(e_ref[j, rows] * d, jnp.sum)
        return du

    du = lax.fori_loop(0, RET, pgrad, du, unroll=4)
    delta = jnp.sum(du, axis=0, keepdims=True) * rl
    fa = rl * SCALE
    fb = fa * delta

    tn = (((0,), (0,)), ((), ()))
    dso = (eo_ref[...] * (dpo_ref[...] * fa - fb)).astype(BF)
    dqt[...] = lax.dot_general(ownx[0], dso, tn, preferred_element_type=F32)
    dko = mm(dso, qs[...])

    def sgrad(j, _):
        ds = (e_ref[j] * (dp_ref[j] * fa - fb)).astype(BF)
        ds_ref[j] = ds
        dqt[...] += lax.dot_general(arrk[pos[j]], ds, tn, preferred_element_type=F32)
        return 0

    lax.fori_loop(0, RET, sgrad, 0, unroll=4)

    give_all(0)

    load_w.wait()
    dqb = jnp.concatenate(
        [dqt[:, h * 128:(h + 1) * 128].T.astype(BF) for h in range(HD)], axis=1
    )

    def project(n, _):
        wn = wv[pl.ds(pl.multiple_of(n * CBW, CBW), CBW), :]
        part = lax.dot_general(
            dqb, wn, (((1,), (1,)), ((), ())), preferred_element_type=F32
        )
        rows = pl.ds(pl.multiple_of(n * 16, 16), 16)
        for dz in range(8):
            for core in range(2):
                block = part[(2 * dz + core) * 8:(2 * dz + core) * 8 + 8]
                both = jnp.concatenate([block[:, :512], block[:, 512:]], axis=0)
                zall[core, dz, rows, :] = both.astype(BF)
        return 0

    def swap_z(h):
        rows = pl.ds(64 * h, 64)
        return rcopy(
            zall.at[1 - c, :, rows], zgot.at[:, rows], pre_s.at[3 + h], pre_r.at[3 + h], (o, mate)
        )

    for h in range(2):
        lax.fori_loop(h * 4, h * 4 + 4, project, 0)
        swap_z(h).start()

    is0 = c == 0
    ogive[...] = jnp.where(is0, dvo, dko).astype(BF)
    own_give = rcopy(ogive, ogot, pre_s.at[2], pre_r.at[2], (o, mate))
    own_give.start()
    own_keep = jnp.where(is0, dko, dvo)

    def term(dist, h):
        at = lax.rem(zi + dist + 8, 8)
        rows = pl.ds(64 * h, 64)
        return zall[c, at, rows].astype(F32) + zgot[at, rows].astype(F32)

    def chain(way, step, h):
        rows = pl.ds(64 * h, 64)
        return rcopy(
            zsnd.at[way, step, rows], zrcv.at[way, step, rows],
            z_s.at[way, 2 * step + h], z_r.at[way, 2 * step + h],
            (o, zup if way == 0 else zdn),
        )

    def chain_step(step, same):
        for way in range(2):
            h = way if same else 1 - way
            rows = pl.ds(64 * h, 64)
            mine = term((1 - 2 * way) * (4 - step), h)
            if step > (0 if same else 1):
                chain(way, step - 1, h).wait_recv()
                mine = mine + zrcv[way, step - 1, rows].astype(F32)
            zsnd[way, step, rows] = mine.astype(BF)
            chain(way, step, h).start()

    for h in range(2):
        swap_z(h).wait_recv()
    chain_step(0, True)
    chain_step(1, False)
    return_part(0, 0)
    chain_step(1, True)
    return_part(0, 1)
    chain_step(2, False)
    return_part(0, 2)
    chain_step(2, True)
    return_part(0, 3)
    chain_step(3, False)
    own_give.wait_recv()
    og_ref[...] = (own_keep + ogot[...].astype(F32)).astype(BF)
    chain_step(3, True)
    for h in range(2):
        total = term(0, h)
        for way in (1 - h, h):
            chain(way, 3, h).wait_recv()
            total = total + zrcv[way, 3, pl.ds(64 * h, 64)].astype(F32)
        for n in range(4):
            for m in range(2):
                at = (h * 4 + n) * CBW + m * 512
                gi_ref[:, at:at + 512] = total[n * 16 + m * 8:n * 16 + m * 8 + 8].astype(BF)

    for k in range(2):
        pl.when(c == k)(swap_kv(k).wait_send)

    def drain(n, _):
        for k in range(2):
            hop(k, n).wait_send()
        return 0

    lax.fori_loop(0, 15, drain, 0)

    def drain2(p, _):
        for k in range(2):
            relay_copy(k, p, c).wait_send()

            @pl.when((p != 15) | (c != k))
            def _():
                home(k, p).wait_send()

            @pl.when((p == 15) & (c == k))
            def _():
                home_self(k).wait()

        for r in range(2):
            @pl.when((p != o) | (c != r))
            def _():
                rcopy(
                    sret.at[0, p], ret_ref.at[r * OWN + p], t_s.at[0, p], t_r.at[r * OWN + p],
                    (o, mate),
                ).wait_recv()

        return 0

    lax.fori_loop(0, OWN, drain2, 0)
    for k in range(2):
        for n in range(4):
            give_copy(k, n).wait_send()
    own_give.wait_send()
    for h in range(2):
        swap_z(h).wait_send()
    for way in range(2):
        for step in range(4):
            for h in range(2):
                if step > 0 or h == way:
                    chain(way, step, h).wait_send()


def add_kernel(
    tab_in, ret_in, gi_in, og_in, out_ref, gi_out, og_out, tab, ret, acc, outv, giv, ogv, sems
):
    get_tab = pltpu.make_async_copy(tab_in, tab, sems.at[0])
    get_tab.start()
    parts = [
        pltpu.make_async_copy(ret_in.at[pl.ds(8 * n, 8)], ret.at[pl.ds(8 * n, 8)], sems.at[1 + n])
        for n in range(4)
    ]
    for copy in parts:
        copy.start()
    fetch = [
        pltpu.make_async_copy(gi_in, giv, sems.at[5]),
        pltpu.make_async_copy(og_in, ogv, sems.at[6]),
    ]
    for copy in fetch:
        copy.start()
    acc[...] = jnp.zeros_like(acc)
    get_tab.wait()
    for copy in fetch:
        copy.wait()
    rest = [
        pltpu.make_async_copy(giv, gi_out, sems.at[5]),
        pltpu.make_async_copy(ogv, og_out, sems.at[6]),
    ]
    for copy in rest:
        copy.start()
    for n in range(4):
        parts[n].wait()

        def step(m, _):
            i = n * 8 + m
            at = tab[2 * lax.rem(i, OWN) + i // OWN]

            @pl.when(at >= 0)
            def _():
                acc[at] += ret[i].astype(F32)

            return 0

        lax.fori_loop(0, 8, step, 0)
    done = []
    for n in range(4):
        part = pl.ds(4 * n, 4)
        outv[part] = acc[part].astype(BF)
        done.append(pltpu.make_async_copy(outv.at[part], out_ref.at[part], sems.at[7 + n]))
        done[-1].start()
    for copy in rest + done:
        copy.wait()


def body(queries, out_grad, own_kv, passage_kv, query_weight, retrieval, passage_slot, passage_blocks):
    vm = pl.BlockSpec(memory_space=pltpu.VMEM)
    sm = pl.BlockSpec(memory_space=pltpu.SMEM)
    hb = pl.BlockSpec(memory_space=pltpu.HBM)
    block = (PLEN, HS)
    dma = pltpu.SemaphoreType.DMA
    gi, og, ret, tab = pl.pallas_call(
        main_kernel,
        out_shape=(
            jax.ShapeDtypeStruct((8, 8192), BF),
            jax.ShapeDtypeStruct((128, HS), BF),
            jax.ShapeDtypeStruct((2 * OWN,) + block, BF),
            jax.ShapeDtypeStruct((2 * OWN,), jnp.int32),
        ),
        in_specs=[hb] * 8,
        out_specs=(vm, vm, hb, sm),
        scratch_shapes=[
            pltpu.SMEM((RET, OWN), jnp.int32),
            pltpu.SMEM((RET * OWN,), jnp.int32),
            pltpu.SMEM((RET * OWN,), jnp.int32),
            pltpu.VMEM((128, ROWS), BF),
            pltpu.VMEM((128, ROWS), BF),
            pltpu.VMEM((OWN,) + block, BF),
            pltpu.VMEM((OWN,) + block, BF),
            pltpu.VMEM((2, 128, HS), BF),
            pltpu.VMEM((2, OWN) + block, BF),
            pltpu.VMEM((2 * OWN,) + block, BF),
            pltpu.VMEM((2 * OWN,) + block, BF),
            pltpu.VMEM((RET, PLEN, ROWS), F32),
            pltpu.VMEM((128, ROWS), F32),
            pltpu.VMEM((RET, PLEN, ROWS), F32),
            pltpu.VMEM((128, ROWS), F32),
            pltpu.VMEM((RET, PLEN, ROWS), BF),
            pltpu.VMEM((ROWS, HS), BF),
            pltpu.VMEM((HS, ROWS), BF),
            pltpu.VMEM((ROWS, HS), BF),
            pltpu.VMEM((HS, ROWS), BF),
            pltpu.VMEM((ROWS, HS), BF),
            pltpu.VMEM((RET,) + block, F32),
            pltpu.VMEM((HS, ROWS), F32),
            pltpu.VMEM((2, OWN) + block, BF),
            pltpu.VMEM((2, OWN) + block, BF),
            pltpu.VMEM((2, OWN) + block, BF),
            pltpu.VMEM((8192, 512), BF),
            pltpu.VMEM((2, 8, 128, 512), BF),
            pltpu.VMEM((8, 128, 512), BF),
            pltpu.VMEM((2, 4, 128, 512), BF),
            pltpu.VMEM((2, 4, 128, 512), BF),
            pltpu.VMEM((128, HS), BF),
            pltpu.VMEM((128, HS), BF),
            pltpu.SMEM((RET,), jnp.int32),
            pltpu.SMEM((2 * OWN,), jnp.int32),
            dma((5,)), dma((5,)),
            dma((2, OWN)), dma((2, OWN)),
            dma((2, OWN)), dma((2, OWN)),
            dma((2, 4)), dma((2, 4)),
            dma((2, OWN)), dma((2 * OWN,)),
            dma((2, 8)), dma((2, 8)),
            dma((8,)),
        ],
        compiler_params=pltpu.CompilerParams(
            collective_id=0, has_side_effects=True, vmem_limit_bytes=60 * 1024 * 1024
        ),
        cost_estimate=pl.CostEstimate(flops=4_000_000_000, bytes_accessed=12_000_000, transcendentals=2_000_000),
        name="exchange_attend",
    )(
        retrieval, passage_slot, passage_blocks, queries, out_grad,
        own_kv.reshape(128, HS), passage_kv.reshape((OWN,) + block), query_weight,
    )
    pg, gi, og = pl.pallas_call(
        add_kernel,
        out_shape=(
            jax.ShapeDtypeStruct((OWN,) + block, BF),
            jax.ShapeDtypeStruct((8, 8192), BF),
            jax.ShapeDtypeStruct((128, HS), BF),
        ),
        in_specs=[hb] * 4,
        out_specs=(hb, hb, hb),
        scratch_shapes=[
            pltpu.SMEM((2 * OWN,), jnp.int32),
            pltpu.VMEM((2 * OWN,) + block, BF),
            pltpu.VMEM((OWN,) + block, F32),
            pltpu.VMEM((OWN,) + block, BF),
            pltpu.VMEM((8, 8192), BF),
            pltpu.VMEM((128, HS), BF),
            dma((11,)),
        ],
        compiler_params=pltpu.CompilerParams(vmem_limit_bytes=60 * 1024 * 1024),
        name="add_returns",
    )(tab, ret, gi, og)
    return gi, pg.reshape((OWN, 1) + block), og.reshape(128, 1, HS)


def solution(mesh):
    placed = (
        P("owner", "tp"),
        P("owner", "tp"),
        P("owner", "tp", None),
        P("owner", "tp", None, None),
        P(None, "tp"),
        P(),
        P(),
        P(),
    )
    return jax.shard_map(
        body,
        mesh=mesh,
        in_specs=placed,
        out_specs=(P(("owner", "tp"), None), P("owner", "tp", None, None), P("owner", "tp", None)),
        check_vma=False,
    )
```

```python
import functools
import math

import jax
import jax.numpy as jnp
from jax import lax
from jax.experimental import pallas as pl
from jax.experimental.pallas import tpu as pltpu
from jax.sharding import PartitionSpec as P

MESH = pl.DeviceIdType.MESH
BF = jnp.bfloat16
F32 = jnp.float32
MASKED = -1e30
OWN = 16
RET = 16
PLEN = 256
HS = 128
HD = 4
ROWS = 512
SCALE = HS ** -0.5
LOG2E = 1.0 / math.log(2.0)
CB = 8
CBW = 1024


def mm(a, b):
    return lax.dot_general(a, b, (((1,), (0,)), ((), ())), preferred_element_type=F32)


def fold(x, op):
    return op(x.reshape(x.shape[0] // 8, 8, x.shape[1]), axis=0)


def main_kernel(
    retr_in, pslot_in, pblk_in, q_in, do_in, own_in, pkv_ref, w_ref,
    gi_ref, og_ref, ret_ref, tab_ref,
    retr, pslot, pblk, q_ref, do_ref,
    kloc, vloc, ownx, snd, arrk, arrv, e_ref, eo_ref, dp_ref, dpo_ref, ds_ref, qs, qt, dos, dot_,
    dosn, dkv, dqt, give, got, sret, wv, zall, zgot, zsnd, zrcv, ogive, ogot,
    pos, inv, pre_s, pre_r, a_s, a_r, b_s, b_r, g_s, g_r, t_s, t_r, z_s, z_r, misc,
):
    o = lax.axis_index("owner")
    t = lax.axis_index("tp")
    c = lax.rem(t, 2)
    zi = t // 2
    mate = t + 1 - 2 * c
    arr = (arrk, arrv)
    loc = (kloc, vloc)

    def rcopy(src, dst, ss, rs, dev):
        return pltpu.make_async_remote_copy(
            src_ref=src, dst_ref=dst, send_sem=ss, recv_sem=rs, device_id=dev, device_id_type=MESH
        )

    def load_kv(k):
        return pltpu.make_async_copy(pkv_ref, loc[k], misc.at[0])

    load_w = pltpu.make_async_copy(w_ref, wv, misc.at[1])
    small = [
        pltpu.make_async_copy(src, dst, misc.at[2 + n])
        for n, (src, dst) in enumerate(
            ((pslot_in, pslot), (retr_in, retr), (pblk_in, pblk),
             (own_in, ownx.at[c]), (q_in, q_ref), (do_in, do_ref))
        )
    ]
    for copy in small[:2]:
        copy.start()
    for k in range(2):
        pl.when(c == k)(load_kv(k).start)

    def shift(n):
        m = jnp.where(n >= 15, 10, n + (n >= 10).astype(jnp.int32))
        return lax.rem(m + 2, 4), lax.rem(m // 4 + 2, 4)

    def peer(n):
        dx, dy = shift(n)
        return lax.rem(o // 4 + dy, 4) * 4 + lax.rem(lax.rem(o, 4) + dx, 4)

    def origin(n):
        dx, dy = shift(n)
        return lax.rem(o // 4 - dy + 4, 4) * 4 + lax.rem(lax.rem(o, 4) - dx + 4, 4)

    bar = pltpu.get_barrier_semaphore()

    def greet(n, _):
        s = peer(n)
        pl.semaphore_signal(bar, inc=1, device_id=(s, t), device_id_type=MESH)
        pl.semaphore_signal(bar, inc=1, device_id=(s, mate), device_id_type=MESH)
        return 0

    lax.fori_loop(0, 15, greet, 0)
    zup = lax.rem(zi + 1, 8) * 2 + c
    zdn = lax.rem(zi + 7, 8) * 2 + c
    for dev in (mate, zup, zdn):
        pl.semaphore_signal(bar, inc=1, device_id=(o, dev), device_id_type=MESH)
    for copy in small[2:]:
        copy.start()
    load_w.start()
    for copy in small[:2]:
        copy.wait()

    def table(s, _):
        first = jnp.int32(-1)
        second = jnp.int32(-1)
        for j in range(RET):
            slot = pslot[retr[s, j]]
            hit = (slot >> 4) == o
            local = slot & 15
            second = jnp.where(hit & (first >= 0), local, second)
            first = jnp.where(hit & (first < 0), local, first)
        tab_ref[2 * s] = first
        tab_ref[2 * s + 1] = second
        return 0

    lax.fori_loop(0, OWN, table, 0)
    small[3].wait()
    pl.semaphore_wait(bar, 33)

    own_x = rcopy(ownx.at[c], ownx.at[c], pre_s.at[1], pre_r.at[1], (o, mate))

    def swap_kv(k):
        return rcopy(loc[k], loc[k], pre_s.at[0], pre_r.at[0], (o, mate))

    def hop(k, n):
        return rcopy(
            snd.at[k, n], arr[k].at[c * OWN + o], a_s.at[k, n], a_r.at[k, o], (peer(n), t)
        )

    def send(k, lo, hi):
        def step(n, _):
            at = jnp.maximum(tab_ref[2 * peer(n) + c], 0)
            snd[k, n] = loc[k][at]
            hop(k, n).start()
            return 0

        lax.fori_loop(lo, hi, step, 0)

    def relay_copy(k, p, core):
        at = core * OWN + p
        return rcopy(arr[k].at[at], arr[k].at[at], b_s.at[k, p], b_r.at[k, p], (o, mate))

    def keep_own(k):
        arr[k][c * OWN + o] = loc[k][jnp.maximum(tab_ref[2 * o + c], 0)]
        relay_copy(k, o, c).start()

    @pl.when(c == 0)
    def _():
        load_kv(0).wait()
        swap_kv(0).start()
        own_x.start()
        send(0, 0, 15)
        keep_own(0)
        swap_kv(1).wait_recv()
        keep_own(1)

    @pl.when(c == 1)
    def _():
        load_kv(1).wait()
        swap_kv(1).start()
        own_x.start()
        send(1, 0, 3)
        swap_kv(0).wait_recv()
        send(0, 0, 15)
        keep_own(0)
        keep_own(1)

    owners = []
    for j in range(RET):
        ow = pslot[retr[o, j]] >> 4
        rank = jnp.int32(0)
        for prev in owners:
            rank = rank + (prev == ow).astype(jnp.int32)
        owners.append(ow)
        pos[j] = jnp.minimum(rank, 1) * OWN + ow

    def inverse(n, _):
        at = jnp.int32(0)
        for j in range(RET):
            at = jnp.where(pos[j] == n, j, at)
        inv[n] = at
        return 0

    lax.fori_loop(0, 2 * OWN, inverse, 0)

    for copy in small[4:]:
        copy.wait()
    for h in range(HD):
        rows = pl.ds(h * 128, 128)
        qh = q_ref[:, h * 128:(h + 1) * 128]
        dh = do_ref[:, h * 128:(h + 1) * 128]
        qs[rows, :] = qh
        dos[rows, :] = dh
        qt[:, rows] = qh.T
        dot_[:, rows] = dh.T
    own_x.wait()
    small[2].wait()

    def relay(k, lo, hi):
        def step(n, _):
            p = origin(n)
            rcopy(
                snd.at[k, 1], arr[k].at[c * OWN + p], a_s.at[k, 1], a_r.at[k, p], (o, mate)
            ).wait_recv()
            relay_copy(k, p, c).start()
            return 0

        lax.fori_loop(lo, hi, step, 0)

    def relays_done(k):
        def step(p, _):
            relay_copy(k, p, 1 - c).wait_recv()
            return 0

        lax.fori_loop(0, OWN, step, 0)

    key_at = lax.broadcasted_iota(jnp.int32, (128, ROWS), 0)
    tok_at = lax.rem(lax.broadcasted_iota(jnp.int32, (128, ROWS), 1), 128)
    so = jnp.where(key_at <= tok_at, mm(ownx[0], qt[...]), MASKED)
    eo_ref[...] = so
    dpo_ref[...] = mm(ownx[1], dot_[...])
    top = fold(so, jnp.max)

    relay(0, 0, 3)
    pl.when(c == 0)(lambda: send(1, 0, 3))
    for n in range(6):
        relay(0, 3 + 2 * n, 5 + 2 * n)
        send(1, 3 + 2 * n, 5 + 2 * n)
    relays_done(0)

    def score(j, top):
        long = pblk[retr[o, j]] >= 2
        kj = arrk[pos[j]]
        s0 = mm(kj[:128], qt[...])
        e_ref[j, 0:128] = s0
        s1 = jnp.where(long, mm(kj[128:], qt[...]), MASKED)
        e_ref[j, 128:256] = s1
        return jnp.maximum(top, jnp.maximum(fold(s0, jnp.max), fold(s1, jnp.max)))

    top = lax.fori_loop(0, RET, score, top, unroll=4)
    kk = SCALE * LOG2E
    mrow = jnp.max(top, axis=0, keepdims=True) * kk

    eo = jnp.exp2(eo_ref[...] * kk - mrow)
    eo_ref[...] = eo
    tot = fold(eo, jnp.sum)

    def expo(j, tot):
        for half in range(2):
            rows = pl.ds(half * 128, 128)
            e = jnp.exp2(e_ref[j, rows] * kk - mrow)
            e_ref[j, rows] = e
            tot = tot + fold(e, jnp.sum)
        return tot

    tot = lax.fori_loop(0, RET, expo, tot, unroll=4)
    rl = 1.0 / jnp.sum(tot, axis=0, keepdims=True)
    for h in range(HD):
        rows = pl.ds(h * 128, 128)
        rcol = jnp.broadcast_to(rl[:, h * 128:(h + 1) * 128], (128, 128)).T
        dosn[rows, :] = (dos[rows, :].astype(F32) * rcol).astype(BF)

    def vgrad(j, _):
        dkv[j] = mm(e_ref[j].astype(BF), dosn[...])
        return 0

    relay(1, 0, 3)
    lax.fori_loop(0, RET // 2, vgrad, 0, unroll=4)
    relay(1, 3, 6)
    lax.fori_loop(RET // 2, RET, vgrad, 0, unroll=4)
    dvo = mm(eo_ref[...].astype(BF), dosn[...])

    def give_copy(k, n):
        part = pl.ds(n * 4, 4)
        return rcopy(
            give.at[k, part], got.at[k, part], g_s.at[k, n], g_r.at[k, n], (o, mate)
        )

    def grads(k, j):
        return dkv[j] if k else mm(ds_ref[j], qs[...])

    def give_all(k):
        def step(n, _):
            for m in range(4):
                i = n * 4 + m
                p = peer(i)
                give[k, i] = grads(k, inv[(1 - c) * OWN + p]).astype(BF)
            give_copy(k, n).start()
            return 0

        lax.fori_loop(0, 4, step, 0)

    def home(k, i):
        return rcopy(
            sret.at[k, i], ret_ref.at[c * OWN + o], t_s.at[k, i], t_r.at[c * OWN + o],
            (peer(i), 2 * zi + k),
        )

    def home_self(k):
        return pltpu.make_async_copy(sret.at[k, 15], ret_ref.at[c * OWN + o], t_s.at[k, 15])

    def return_part(k, n):
        give_copy(k, n).wait_recv()

        def step(m, _):
            i = n * 4 + m
            p = peer(i)
            sret[k, i] = (grads(k, inv[c * OWN + p]) + got[k, i].astype(F32)).astype(BF)

            @pl.when((i != 15) | (c != k))
            def _():
                home(k, i).start()

            @pl.when((i == 15) & (c == k))
            def _():
                home_self(k).start()

            return 0

        lax.fori_loop(0, 4, step, 0, unroll=2)

    give_all(1)
    relay(1, 6, 9)
    for n in range(4):
        return_part(1, n)
    relay(1, 9, 15)
    relays_done(1)

    du = fold(eo_ref[...] * dpo_ref[...], jnp.sum)

    def pgrad(j, du):
        vj = arrv[pos[j]]
        for half in range(2):
            rows = pl.ds(half * 128, 128)
            d = mm(vj[half * 128:(half + 1) * 128], dot_[...])
            dp_ref[j, rows] = d
            du = du + fold(e_ref[j, rows] * d, jnp.sum)
        return du

    du = lax.fori_loop(0, RET, pgrad, du, unroll=4)
    delta = jnp.sum(du, axis=0, keepdims=True) * rl
    fa = rl * SCALE
    fb = fa * delta

    tn = (((0,), (0,)), ((), ()))
    dso = (eo_ref[...] * (dpo_ref[...] * fa - fb)).astype(BF)
    dqt[...] = lax.dot_general(ownx[0], dso, tn, preferred_element_type=F32)
    dko = mm(dso, qs[...])

    def sgrad(j, _):
        ds = (e_ref[j] * (dp_ref[j] * fa - fb)).astype(BF)
        ds_ref[j] = ds
        dqt[...] += lax.dot_general(arrk[pos[j]], ds, tn, preferred_element_type=F32)
        return 0

    lax.fori_loop(0, RET, sgrad, 0, unroll=4)

    give_all(0)

    load_w.wait()
    dqb = jnp.concatenate(
        [dqt[:, h * 128:(h + 1) * 128].T.astype(BF) for h in range(HD)], axis=1
    )

    def project(n, _):
        wn = wv[pl.ds(pl.multiple_of(n * CBW, CBW), CBW), :]
        part = lax.dot_general(
            dqb, wn, (((1,), (1,)), ((), ())), preferred_element_type=F32
        )
        rows = pl.ds(pl.multiple_of(n * 16, 16), 16)
        for dz in range(8):
            for core in range(2):
                block = part[(2 * dz + core) * 8:(2 * dz + core) * 8 + 8]
                both = jnp.concatenate([block[:, :512], block[:, 512:]], axis=0)
                zall[core, dz, rows, :] = both.astype(BF)
        return 0

    def swap_z(h):
        rows = pl.ds(64 * h, 64)
        return rcopy(
            zall.at[1 - c, :, rows], zgot.at[:, rows], pre_s.at[3 + h], pre_r.at[3 + h], (o, mate)
        )

    for h in range(2):
        lax.fori_loop(h * 4, h * 4 + 4, project, 0, unroll=2)
        swap_z(h).start()

    is0 = c == 0
    ogive[...] = jnp.where(is0, dvo, dko).astype(BF)
    own_give = rcopy(ogive, ogot, pre_s.at[2], pre_r.at[2], (o, mate))
    own_give.start()
    own_keep = jnp.where(is0, dko, dvo)

    def term(dist, h):
        at = lax.rem(zi + dist + 8, 8)
        rows = pl.ds(64 * h, 64)
        return zall[c, at, rows].astype(F32) + zgot[at, rows].astype(F32)

    def chain(way, step, h):
        rows = pl.ds(64 * h, 64)
        return rcopy(
            zsnd.at[way, step, rows], zrcv.at[way, step, rows],
            z_s.at[way, 2 * step + h], z_r.at[way, 2 * step + h],
            (o, zup if way == 0 else zdn),
        )

    def chain_step(step, same):
        for way in range(2):
            h = way if same else 1 - way
            rows = pl.ds(64 * h, 64)
            mine = term((1 - 2 * way) * (4 - step), h)
            if step > (0 if same else 1):
                chain(way, step - 1, h).wait_recv()
                mine = mine + zrcv[way, step - 1, rows].astype(F32)
            zsnd[way, step, rows] = mine.astype(BF)
            chain(way, step, h).start()

    return_part(0, 0)
    return_part(0, 1)
    for h in range(2):
        swap_z(h).wait_recv()
    chain_step(0, True)
    chain_step(1, False)
    return_part(0, 2)
    return_part(0, 3)
    chain_step(1, True)
    chain_step(2, False)
    chain_step(2, True)
    chain_step(3, False)
    own_give.wait_recv()
    og_ref[...] = (own_keep + ogot[...].astype(F32)).astype(BF)
    chain_step(3, True)
    for h in range(2):
        total = term(0, h)
        for way in (1 - h, h):
            chain(way, 3, h).wait_recv()
            total = total + zrcv[way, 3, pl.ds(64 * h, 64)].astype(F32)
        for n in range(4):
            for m in range(2):
                at = (h * 4 + n) * CBW + m * 512
                gi_ref[:, at:at + 512] = total[n * 16 + m * 8:n * 16 + m * 8 + 8].astype(BF)

    for k in range(2):
        pl.when(c == k)(swap_kv(k).wait_send)

    def drain(n, _):
        for k in range(2):
            hop(k, n).wait_send()
        return 0

    lax.fori_loop(0, 15, drain, 0)

    def drain2(p, _):
        for k in range(2):
            relay_copy(k, p, c).wait_send()

            @pl.when((p != 15) | (c != k))
            def _():
                home(k, p).wait_send()

            @pl.when((p == 15) & (c == k))
            def _():
                home_self(k).wait()

        for r in range(2):
            @pl.when((p != o) | (c != r))
            def _():
                rcopy(
                    sret.at[0, p], ret_ref.at[r * OWN + p], t_s.at[0, p], t_r.at[r * OWN + p],
                    (o, mate),
                ).wait_recv()

        return 0

    lax.fori_loop(0, OWN, drain2, 0)
    for k in range(2):
        for n in range(4):
            give_copy(k, n).wait_send()
    own_give.wait_send()
    for h in range(2):
        swap_z(h).wait_send()
    for way in range(2):
        for step in range(4):
            for h in range(2):
                if step > 0 or h == way:
                    chain(way, step, h).wait_send()


def add_kernel(
    tab_in, ret_in, gi_in, og_in, out_ref, gi_out, og_out, tab, ret, acc, outv, giv, ogv, sems
):
    get_tab = pltpu.make_async_copy(tab_in, tab, sems.at[0])
    get_tab.start()
    parts = [
        pltpu.make_async_copy(ret_in.at[pl.ds(8 * n, 8)], ret.at[pl.ds(8 * n, 8)], sems.at[1 + n])
        for n in range(4)
    ]
    for copy in parts:
        copy.start()
    fetch = [
        pltpu.make_async_copy(gi_in, giv, sems.at[5]),
        pltpu.make_async_copy(og_in, ogv, sems.at[6]),
    ]
    for copy in fetch:
        copy.start()
    acc[...] = jnp.zeros_like(acc)
    get_tab.wait()
    for copy in fetch:
        copy.wait()
    rest = [
        pltpu.make_async_copy(giv, gi_out, sems.at[5]),
        pltpu.make_async_copy(ogv, og_out, sems.at[6]),
    ]
    for copy in rest:
        copy.start()
    for n in range(4):
        parts[n].wait()

        def step(m, _):
            i = n * 8 + m
            at = tab[2 * lax.rem(i, OWN) + i // OWN]

            @pl.when(at >= 0)
            def _():
                acc[at] += ret[i].astype(F32)

            return 0

        lax.fori_loop(0, 8, step, 0)
    done = []
    for n in range(4):
        part = pl.ds(4 * n, 4)
        outv[part] = acc[part].astype(BF)
        done.append(pltpu.make_async_copy(outv.at[part], out_ref.at[part], sems.at[7 + n]))
        done[-1].start()
    for copy in rest + done:
        copy.wait()


def body(queries, out_grad, own_kv, passage_kv, query_weight, retrieval, passage_slot, passage_blocks):
    vm = pl.BlockSpec(memory_space=pltpu.VMEM)
    sm = pl.BlockSpec(memory_space=pltpu.SMEM)
    hb = pl.BlockSpec(memory_space=pltpu.HBM)
    block = (PLEN, HS)
    dma = pltpu.SemaphoreType.DMA
    gi, og, ret, tab = pl.pallas_call(
        main_kernel,
        out_shape=(
            jax.ShapeDtypeStruct((8, 8192), BF),
            jax.ShapeDtypeStruct((128, HS), BF),
            jax.ShapeDtypeStruct((2 * OWN,) + block, BF),
            jax.ShapeDtypeStruct((2 * OWN,), jnp.int32),
        ),
        in_specs=[hb] * 8,
        out_specs=(vm, vm, hb, sm),
        scratch_shapes=[
            pltpu.SMEM((RET, OWN), jnp.int32),
            pltpu.SMEM((RET * OWN,), jnp.int32),
            pltpu.SMEM((RET * OWN,), jnp.int32),
            pltpu.VMEM((128, ROWS), BF),
            pltpu.VMEM((128, ROWS), BF),
            pltpu.VMEM((OWN,) + block, BF),
            pltpu.VMEM((OWN,) + block, BF),
            pltpu.VMEM((2, 128, HS), BF),
            pltpu.VMEM((2, OWN) + block, BF),
            pltpu.VMEM((2 * OWN,) + block, BF),
            pltpu.VMEM((2 * OWN,) + block, BF),
            pltpu.VMEM((RET, PLEN, ROWS), F32),
            pltpu.VMEM((128, ROWS), F32),
            pltpu.VMEM((RET, PLEN, ROWS), F32),
            pltpu.VMEM((128, ROWS), F32),
            pltpu.VMEM((RET, PLEN, ROWS), BF),
            pltpu.VMEM((ROWS, HS), BF),
            pltpu.VMEM((HS, ROWS), BF),
            pltpu.VMEM((ROWS, HS), BF),
            pltpu.VMEM((HS, ROWS), BF),
            pltpu.VMEM((ROWS, HS), BF),
            pltpu.VMEM((RET,) + block, F32),
            pltpu.VMEM((HS, ROWS), F32),
            pltpu.VMEM((2, OWN) + block, BF),
            pltpu.VMEM((2, OWN) + block, BF),
            pltpu.VMEM((2, OWN) + block, BF),
            pltpu.VMEM((8192, 512), BF),
            pltpu.VMEM((2, 8, 128, 512), BF),
            pltpu.VMEM((8, 128, 512), BF),
            pltpu.VMEM((2, 4, 128, 512), BF),
            pltpu.VMEM((2, 4, 128, 512), BF),
            pltpu.VMEM((128, HS), BF),
            pltpu.VMEM((128, HS), BF),
            pltpu.SMEM((RET,), jnp.int32),
            pltpu.SMEM((2 * OWN,), jnp.int32),
            dma((5,)), dma((5,)),
            dma((2, OWN)), dma((2, OWN)),
            dma((2, OWN)), dma((2, OWN)),
            dma((2, 4)), dma((2, 4)),
            dma((2, OWN)), dma((2 * OWN,)),
            dma((2, 8)), dma((2, 8)),
            dma((8,)),
        ],
        compiler_params=pltpu.CompilerParams(
            collective_id=0, has_side_effects=True, vmem_limit_bytes=60 * 1024 * 1024
        ),
        cost_estimate=pl.CostEstimate(flops=4_000_000_000, bytes_accessed=12_000_000, transcendentals=2_000_000),
        name="exchange_attend",
    )(
        retrieval, passage_slot, passage_blocks, queries, out_grad,
        own_kv.reshape(128, HS), passage_kv.reshape((OWN,) + block), query_weight,
    )
    pg, gi, og = pl.pallas_call(
        add_kernel,
        out_shape=(
            jax.ShapeDtypeStruct((OWN,) + block, BF),
            jax.ShapeDtypeStruct((8, 8192), BF),
            jax.ShapeDtypeStruct((128, HS), BF),
        ),
        in_specs=[hb] * 4,
        out_specs=(hb, hb, hb),
        scratch_shapes=[
            pltpu.SMEM((2 * OWN,), jnp.int32),
            pltpu.VMEM((2 * OWN,) + block, BF),
            pltpu.VMEM((OWN,) + block, F32),
            pltpu.VMEM((OWN,) + block, BF),
            pltpu.VMEM((8, 8192), BF),
            pltpu.VMEM((128, HS), BF),
            dma((11,)),
        ],
        compiler_params=pltpu.CompilerParams(vmem_limit_bytes=60 * 1024 * 1024),
        name="add_returns",
    )(tab, ret, gi, og)
    return gi, pg.reshape((OWN, 1) + block), og.reshape(128, 1, HS)


def solution(mesh):
    placed = (
        P("owner", "tp"),
        P("owner", "tp"),
        P("owner", "tp", None),
        P("owner", "tp", None, None),
        P(None, "tp"),
        P(),
        P(),
        P(),
    )
    return jax.shard_map(
        body,
        mesh=mesh,
        in_specs=placed,
        out_specs=(P(("owner", "tp"), None), P("owner", "tp", None, None), P("owner", "tp", None)),
        check_vma=False,
    )
```

```python
import functools
import math

import jax
import jax.numpy as jnp
from jax import lax
from jax.experimental import pallas as pl
from jax.experimental.pallas import tpu as pltpu
from jax.sharding import PartitionSpec as P

MESH = pl.DeviceIdType.MESH
BF = jnp.bfloat16
F32 = jnp.float32
MASKED = -1e30
OWN = 16
RET = 16
PLEN = 256
HS = 128
HD = 4
ROWS = 512
SCALE = HS ** -0.5
LOG2E = 1.0 / math.log(2.0)
CB = 8
CBW = 1024


def mm(a, b):
    return lax.dot_general(a, b, (((1,), (0,)), ((), ())), preferred_element_type=F32)


def fold(x, op):
    return op(x.reshape(x.shape[0] // 8, 8, x.shape[1]), axis=0)


def main_kernel(
    retr_in, pslot_in, pblk_in, q_in, do_in, own_in, pkv_ref, w_ref,
    gi_ref, og_ref, ret_ref, tab_ref,
    retr, pslot, pblk, q_ref, do_ref,
    kloc, vloc, ownx, snd, arrk, arrv, e_ref, eo_ref, dp_ref, dpo_ref, ds_ref, qs, qt, dos, dot_,
    dosn, dkv, dqt, give, got, sret, wv, zall, zgot, zsnd, zrcv, ogive, ogot,
    pos, inv, pre_s, pre_r, a_s, a_r, b_s, b_r, g_s, g_r, t_s, t_r, z_s, z_r, misc,
):
    o = lax.axis_index("owner")
    t = lax.axis_index("tp")
    c = lax.rem(t, 2)
    zi = t // 2
    mate = t + 1 - 2 * c
    arr = (arrk, arrv)
    loc = (kloc, vloc)

    def rcopy(src, dst, ss, rs, dev):
        return pltpu.make_async_remote_copy(
            src_ref=src, dst_ref=dst, send_sem=ss, recv_sem=rs, device_id=dev, device_id_type=MESH
        )

    def load_kv(k):
        return pltpu.make_async_copy(pkv_ref, loc[k], misc.at[0])

    load_w = pltpu.make_async_copy(w_ref, wv, misc.at[1])
    small = [
        pltpu.make_async_copy(src, dst, misc.at[2 + n])
        for n, (src, dst) in enumerate(
            ((pslot_in, pslot), (retr_in, retr), (pblk_in, pblk),
             (own_in, ownx.at[c]), (q_in, q_ref), (do_in, do_ref))
        )
    ]
    for copy in small[:2]:
        copy.start()
    for k in range(2):
        pl.when(c == k)(load_kv(k).start)

    def shift(n):
        m = jnp.where(n >= 15, 10, n + (n >= 10).astype(jnp.int32))
        return lax.rem(m + 2, 4), lax.rem(m // 4 + 2, 4)

    def peer(n):
        dx, dy = shift(n)
        return lax.rem(o // 4 + dy, 4) * 4 + lax.rem(lax.rem(o, 4) + dx, 4)

    def origin(n):
        dx, dy = shift(n)
        return lax.rem(o // 4 - dy + 4, 4) * 4 + lax.rem(lax.rem(o, 4) - dx + 4, 4)

    bar = pltpu.get_barrier_semaphore()

    def greet(n, _):
        s = peer(n)
        pl.semaphore_signal(bar, inc=1, device_id=(s, t), device_id_type=MESH)
        pl.semaphore_signal(bar, inc=1, device_id=(s, mate), device_id_type=MESH)
        return 0

    lax.fori_loop(0, 15, greet, 0)
    zup = lax.rem(zi + 1, 8) * 2 + c
    zdn = lax.rem(zi + 7, 8) * 2 + c
    for dev in (mate, zup, zdn):
        pl.semaphore_signal(bar, inc=1, device_id=(o, dev), device_id_type=MESH)
    for copy in small[2:]:
        copy.start()
    load_w.start()
    for copy in small[:2]:
        copy.wait()

    def table(s, _):
        first = jnp.int32(-1)
        second = jnp.int32(-1)
        for j in range(RET):
            slot = pslot[retr[s, j]]
            hit = (slot >> 4) == o
            local = slot & 15
            second = jnp.where(hit & (first >= 0), local, second)
            first = jnp.where(hit & (first < 0), local, first)
        tab_ref[2 * s] = first
        tab_ref[2 * s + 1] = second
        return 0

    lax.fori_loop(0, OWN, table, 0)
    small[3].wait()
    pl.semaphore_wait(bar, 33)

    own_x = rcopy(ownx.at[c], ownx.at[c], pre_s.at[1], pre_r.at[1], (o, mate))

    def swap_kv(k):
        return rcopy(loc[k], loc[k], pre_s.at[0], pre_r.at[0], (o, mate))

    def hop(k, n):
        return rcopy(
            snd.at[k, n], arr[k].at[c * OWN + o], a_s.at[k, n], a_r.at[k, o], (peer(n), t)
        )

    def send(k, lo, hi):
        def step(n, _):
            at = jnp.maximum(tab_ref[2 * peer(n) + c], 0)
            snd[k, n] = loc[k][at]
            hop(k, n).start()
            return 0

        lax.fori_loop(lo, hi, step, 0)

    def relay_copy(k, p, core):
        at = core * OWN + p
        return rcopy(arr[k].at[at], arr[k].at[at], b_s.at[k, p], b_r.at[k, p], (o, mate))

    def keep_own(k):
        arr[k][c * OWN + o] = loc[k][jnp.maximum(tab_ref[2 * o + c], 0)]
        relay_copy(k, o, c).start()

    @pl.when(c == 0)
    def _():
        load_kv(0).wait()
        swap_kv(0).start()
        own_x.start()
        send(0, 0, 15)
        keep_own(0)
        swap_kv(1).wait_recv()
        keep_own(1)

    @pl.when(c == 1)
    def _():
        load_kv(1).wait()
        swap_kv(1).start()
        own_x.start()
        send(1, 0, 3)
        swap_kv(0).wait_recv()
        send(0, 0, 15)
        keep_own(0)
        keep_own(1)

    owners = []
    for j in range(RET):
        ow = pslot[retr[o, j]] >> 4
        rank = jnp.int32(0)
        for prev in owners:
            rank = rank + (prev == ow).astype(jnp.int32)
        owners.append(ow)
        pos[j] = jnp.minimum(rank, 1) * OWN + ow

    def inverse(n, _):
        at = jnp.int32(0)
        for j in range(RET):
            at = jnp.where(pos[j] == n, j, at)
        inv[n] = at
        return 0

    lax.fori_loop(0, 2 * OWN, inverse, 0)

    for copy in small[4:]:
        copy.wait()
    for h in range(HD):
        rows = pl.ds(h * 128, 128)
        qh = q_ref[:, h * 128:(h + 1) * 128]
        dh = do_ref[:, h * 128:(h + 1) * 128]
        qs[rows, :] = qh
        dos[rows, :] = dh
        qt[:, rows] = qh.T
        dot_[:, rows] = dh.T
    own_x.wait()
    small[2].wait()

    def relay(k, lo, hi):
        def step(n, _):
            p = origin(n)
            rcopy(
                snd.at[k, 1], arr[k].at[c * OWN + p], a_s.at[k, 1], a_r.at[k, p], (o, mate)
            ).wait_recv()
            relay_copy(k, p, c).start()
            return 0

        lax.fori_loop(lo, hi, step, 0)

    def relays_done(k):
        def step(p, _):
            relay_copy(k, p, 1 - c).wait_recv()
            return 0

        lax.fori_loop(0, OWN, step, 0)

    key_at = lax.broadcasted_iota(jnp.int32, (128, ROWS), 0)
    tok_at = lax.rem(lax.broadcasted_iota(jnp.int32, (128, ROWS), 1), 128)
    so = jnp.where(key_at <= tok_at, mm(ownx[0], qt[...]), MASKED)
    eo_ref[...] = so
    dpo_ref[...] = mm(ownx[1], dot_[...])
    top = fold(so, jnp.max)

    relay(0, 0, 3)
    pl.when(c == 0)(lambda: send(1, 0, 3))
    for n in range(6):
        relay(0, 3 + 2 * n, 5 + 2 * n)
        send(1, 3 + 2 * n, 5 + 2 * n)
    relays_done(0)

    def score(j, top):
        long = pblk[retr[o, j]] >= 2
        kj = arrk[pos[j]]
        s0 = mm(kj[:128], qt[...])
        e_ref[j, 0:128] = s0
        s1 = jnp.where(long, mm(kj[128:], qt[...]), MASKED)
        e_ref[j, 128:256] = s1
        return jnp.maximum(top, jnp.maximum(fold(s0, jnp.max), fold(s1, jnp.max)))

    top = lax.fori_loop(0, RET, score, top, unroll=4)
    kk = SCALE * LOG2E
    mrow = jnp.max(top, axis=0, keepdims=True) * kk

    eo = jnp.exp2(eo_ref[...] * kk - mrow)
    eo_ref[...] = eo
    tot = fold(eo, jnp.sum)

    def expo(j, tot):
        for half in range(2):
            rows = pl.ds(half * 128, 128)
            e = jnp.exp2(e_ref[j, rows] * kk - mrow)
            e_ref[j, rows] = e
            tot = tot + fold(e, jnp.sum)
        return tot

    tot = lax.fori_loop(0, RET, expo, tot, unroll=4)
    rl = 1.0 / jnp.sum(tot, axis=0, keepdims=True)
    for h in range(HD):
        rows = pl.ds(h * 128, 128)
        rcol = jnp.broadcast_to(rl[:, h * 128:(h + 1) * 128], (128, 128)).T
        dosn[rows, :] = (dos[rows, :].astype(F32) * rcol).astype(BF)

    def vgrad(j, _):
        dkv[j] = mm(e_ref[j].astype(BF), dosn[...])
        return 0

    relay(1, 0, 3)
    lax.fori_loop(0, RET // 2, vgrad, 0, unroll=4)
    relay(1, 3, 6)
    lax.fori_loop(RET // 2, RET, vgrad, 0, unroll=4)
    dvo = mm(eo_ref[...].astype(BF), dosn[...])

    def give_copy(k, n):
        part = pl.ds(n * 4, 4)
        return rcopy(
            give.at[k, part], got.at[k, part], g_s.at[k, n], g_r.at[k, n], (o, mate)
        )

    def grads(k, j):
        return dkv[j] if k else mm(ds_ref[j], qs[...])

    def give_all(k):
        def step(n, _):
            for m in range(4):
                i = n * 4 + m
                p = peer(i)
                give[k, i] = grads(k, inv[(1 - c) * OWN + p]).astype(BF)
            give_copy(k, n).start()
            return 0

        lax.fori_loop(0, 4, step, 0)

    def home(k, i):
        return rcopy(
            sret.at[k, i], ret_ref.at[c * OWN + o], t_s.at[k, i], t_r.at[c * OWN + o],
            (peer(i), 2 * zi + k),
        )

    def home_self(k):
        return pltpu.make_async_copy(sret.at[k, 15], ret_ref.at[c * OWN + o], t_s.at[k, 15])

    def return_part(k, n):
        give_copy(k, n).wait_recv()

        def step(m, _):
            i = n * 4 + m
            p = peer(i)
            sret[k, i] = (grads(k, inv[c * OWN + p]) + got[k, i].astype(F32)).astype(BF)

            @pl.when((i != 15) | (c != k))
            def _():
                home(k, i).start()

            @pl.when((i == 15) & (c == k))
            def _():
                home_self(k).start()

            return 0

        lax.fori_loop(0, 4, step, 0, unroll=2)

    give_all(1)
    relay(1, 6, 9)
    for n in range(4):
        return_part(1, n)
    relay(1, 9, 15)
    relays_done(1)

    du = fold(eo_ref[...] * dpo_ref[...], jnp.sum)

    def pgrad(j, du):
        vj = arrv[pos[j]]
        for half in range(2):
            rows = pl.ds(half * 128, 128)
            d = mm(vj[half * 128:(half + 1) * 128], dot_[...])
            dp_ref[j, rows] = d
            du = du + fold(e_ref[j, rows] * d, jnp.sum)
        return du

    du = lax.fori_loop(0, RET, pgrad, du, unroll=4)
    delta = jnp.sum(du, axis=0, keepdims=True) * rl
    fa = rl * SCALE
    fb = fa * delta

    tn = (((0,), (0,)), ((), ()))
    dso = (eo_ref[...] * (dpo_ref[...] * fa - fb)).astype(BF)
    dqt[...] = lax.dot_general(ownx[0], dso, tn, preferred_element_type=F32)
    dko = mm(dso, qs[...])

    def sgrad(j, _):
        ds = (e_ref[j] * (dp_ref[j] * fa - fb)).astype(BF)
        ds_ref[j] = ds
        dqt[...] += lax.dot_general(arrk[pos[j]], ds, tn, preferred_element_type=F32)
        return 0

    lax.fori_loop(0, RET, sgrad, 0, unroll=4)

    load_w.wait()
    dqb = jnp.concatenate(
        [dqt[:, h * 128:(h + 1) * 128].T.astype(BF) for h in range(HD)], axis=1
    )

    def project(n, _):
        wn = wv[pl.ds(pl.multiple_of(n * CBW, CBW), CBW), :]
        part = lax.dot_general(
            dqb, wn, (((1,), (1,)), ((), ())), preferred_element_type=F32
        )
        rows = pl.ds(pl.multiple_of(n * 16, 16), 16)
        for dz in range(8):
            for core in range(2):
                block = part[(2 * dz + core) * 8:(2 * dz + core) * 8 + 8]
                both = jnp.concatenate([block[:, :512], block[:, 512:]], axis=0)
                zall[core, dz, rows, :] = both.astype(BF)
        return 0

    def swap_z(h):
        rows = pl.ds(64 * h, 64)
        return rcopy(
            zall.at[1 - c, :, rows], zgot.at[:, rows], pre_s.at[3 + h], pre_r.at[3 + h], (o, mate)
        )

    for h in range(2):
        lax.fori_loop(h * 4, h * 4 + 4, project, 0)
        swap_z(h).start()

    is0 = c == 0
    ogive[...] = jnp.where(is0, dvo, dko).astype(BF)
    own_give = rcopy(ogive, ogot, pre_s.at[2], pre_r.at[2], (o, mate))
    own_give.start()
    own_keep = jnp.where(is0, dko, dvo)

    give_all(0)

    def term(dist, h):
        at = lax.rem(zi + dist + 8, 8)
        rows = pl.ds(64 * h, 64)
        return zall[c, at, rows].astype(F32) + zgot[at, rows].astype(F32)

    def chain(way, step, h):
        rows = pl.ds(64 * h, 64)
        return rcopy(
            zsnd.at[way, step, rows], zrcv.at[way, step, rows],
            z_s.at[way, 2 * step + h], z_r.at[way, 2 * step + h],
            (o, zup if way == 0 else zdn),
        )

    def chain_step(step, same):
        for way in range(2):
            h = way if same else 1 - way
            rows = pl.ds(64 * h, 64)
            mine = term((1 - 2 * way) * (4 - step), h)
            if step > (0 if same else 1):
                chain(way, step - 1, h).wait_recv()
                mine = mine + zrcv[way, step - 1, rows].astype(F32)
            zsnd[way, step, rows] = mine.astype(BF)
            chain(way, step, h).start()

    for h in range(2):
        swap_z(h).wait_recv()
    chain_step(0, True)
    chain_step(1, False)
    return_part(0, 0)
    chain_step(1, True)
    return_part(0, 1)
    chain_step(2, False)
    return_part(0, 2)
    chain_step(2, True)
    return_part(0, 3)
    chain_step(3, False)
    own_give.wait_recv()
    og_ref[...] = (own_keep + ogot[...].astype(F32)).astype(BF)
    chain_step(3, True)
    for h in range(2):
        total = term(0, h)
        for way in (1 - h, h):
            chain(way, 3, h).wait_recv()
            total = total + zrcv[way, 3, pl.ds(64 * h, 64)].astype(F32)
        for n in range(4):
            for m in range(2):
                at = (h * 4 + n) * CBW + m * 512
                gi_ref[:, at:at + 512] = total[n * 16 + m * 8:n * 16 + m * 8 + 8].astype(BF)

    for k in range(2):
        pl.when(c == k)(swap_kv(k).wait_send)

    def drain(n, _):
        for k in range(2):
            hop(k, n).wait_send()
        return 0

    lax.fori_loop(0, 15, drain, 0)

    def drain2(p, _):
        for k in range(2):
            relay_copy(k, p, c).wait_send()

            @pl.when((p != 15) | (c != k))
            def _():
                home(k, p).wait_send()

            @pl.when((p == 15) & (c == k))
            def _():
                home_self(k).wait()

        for r in range(2):
            @pl.when((p != o) | (c != r))
            def _():
                rcopy(
                    sret.at[0, p], ret_ref.at[r * OWN + p], t_s.at[0, p], t_r.at[r * OWN + p],
                    (o, mate),
                ).wait_recv()

        return 0

    lax.fori_loop(0, OWN, drain2, 0)
    for k in range(2):
        for n in range(4):
            give_copy(k, n).wait_send()
    own_give.wait_send()
    for h in range(2):
        swap_z(h).wait_send()
    for way in range(2):
        for step in range(4):
            for h in range(2):
                if step > 0 or h == way:
                    chain(way, step, h).wait_send()


def add_kernel(
    tab_in, ret_in, gi_in, og_in, out_ref, gi_out, og_out, tab, ret, acc, outv, giv, ogv, sems
):
    get_tab = pltpu.make_async_copy(tab_in, tab, sems.at[0])
    get_tab.start()
    parts = [
        pltpu.make_async_copy(ret_in.at[pl.ds(8 * n, 8)], ret.at[pl.ds(8 * n, 8)], sems.at[1 + n])
        for n in range(4)
    ]
    for copy in parts:
        copy.start()
    fetch = [
        pltpu.make_async_copy(gi_in, giv, sems.at[5]),
        pltpu.make_async_copy(og_in, ogv, sems.at[6]),
    ]
    for copy in fetch:
        copy.start()
    acc[...] = jnp.zeros_like(acc)
    get_tab.wait()
    for copy in fetch:
        copy.wait()
    rest = [
        pltpu.make_async_copy(giv, gi_out, sems.at[5]),
        pltpu.make_async_copy(ogv, og_out, sems.at[6]),
    ]
    for copy in rest:
        copy.start()
    for n in range(4):
        parts[n].wait()

        def step(m, _):
            i = n * 8 + m
            at = tab[2 * lax.rem(i, OWN) + i // OWN]

            @pl.when(at >= 0)
            def _():
                acc[at] += ret[i].astype(F32)

            return 0

        lax.fori_loop(0, 8, step, 0)
    done = []
    for n in range(4):
        part = pl.ds(4 * n, 4)
        outv[part] = acc[part].astype(BF)
        done.append(pltpu.make_async_copy(outv.at[part], out_ref.at[part], sems.at[7 + n]))
        done[-1].start()
    for copy in rest + done:
        copy.wait()


def body(queries, out_grad, own_kv, passage_kv, query_weight, retrieval, passage_slot, passage_blocks):
    vm = pl.BlockSpec(memory_space=pltpu.VMEM)
    sm = pl.BlockSpec(memory_space=pltpu.SMEM)
    hb = pl.BlockSpec(memory_space=pltpu.HBM)
    block = (PLEN, HS)
    dma = pltpu.SemaphoreType.DMA
    gi, og, ret, tab = pl.pallas_call(
        main_kernel,
        out_shape=(
            jax.ShapeDtypeStruct((8, 8192), BF),
            jax.ShapeDtypeStruct((128, HS), BF),
            jax.ShapeDtypeStruct((2 * OWN,) + block, BF),
            jax.ShapeDtypeStruct((2 * OWN,), jnp.int32),
        ),
        in_specs=[hb] * 8,
        out_specs=(vm, vm, hb, sm),
        scratch_shapes=[
            pltpu.SMEM((RET, OWN), jnp.int32),
            pltpu.SMEM((RET * OWN,), jnp.int32),
            pltpu.SMEM((RET * OWN,), jnp.int32),
            pltpu.VMEM((128, ROWS), BF),
            pltpu.VMEM((128, ROWS), BF),
            pltpu.VMEM((OWN,) + block, BF),
            pltpu.VMEM((OWN,) + block, BF),
            pltpu.VMEM((2, 128, HS), BF),
            pltpu.VMEM((2, OWN) + block, BF),
            pltpu.VMEM((2 * OWN,) + block, BF),
            pltpu.VMEM((2 * OWN,) + block, BF),
            pltpu.VMEM((RET, PLEN, ROWS), F32),
            pltpu.VMEM((128, ROWS), F32),
            pltpu.VMEM((RET, PLEN, ROWS), F32),
            pltpu.VMEM((128, ROWS), F32),
            pltpu.VMEM((RET, PLEN, ROWS), BF),
            pltpu.VMEM((ROWS, HS), BF),
            pltpu.VMEM((HS, ROWS), BF),
            pltpu.VMEM((ROWS, HS), BF),
            pltpu.VMEM((HS, ROWS), BF),
            pltpu.VMEM((ROWS, HS), BF),
            pltpu.VMEM((RET,) + block, F32),
            pltpu.VMEM((HS, ROWS), F32),
            pltpu.VMEM((2, OWN) + block, BF),
            pltpu.VMEM((2, OWN) + block, BF),
            pltpu.VMEM((2, OWN) + block, BF),
            pltpu.VMEM((8192, 512), BF),
            pltpu.VMEM((2, 8, 128, 512), BF),
            pltpu.VMEM((8, 128, 512), BF),
            pltpu.VMEM((2, 4, 128, 512), BF),
            pltpu.VMEM((2, 4, 128, 512), BF),
            pltpu.VMEM((128, HS), BF),
            pltpu.VMEM((128, HS), BF),
            pltpu.SMEM((RET,), jnp.int32),
            pltpu.SMEM((2 * OWN,), jnp.int32),
            dma((5,)), dma((5,)),
            dma((2, OWN)), dma((2, OWN)),
            dma((2, OWN)), dma((2, OWN)),
            dma((2, 4)), dma((2, 4)),
            dma((2, OWN)), dma((2 * OWN,)),
            dma((2, 8)), dma((2, 8)),
            dma((8,)),
        ],
        compiler_params=pltpu.CompilerParams(
            collective_id=0, has_side_effects=True, vmem_limit_bytes=60 * 1024 * 1024
        ),
        cost_estimate=pl.CostEstimate(flops=4_000_000_000, bytes_accessed=12_000_000, transcendentals=2_000_000),
        name="exchange_attend",
    )(
        retrieval, passage_slot, passage_blocks, queries, out_grad,
        own_kv.reshape(128, HS), passage_kv.reshape((OWN,) + block), query_weight,
    )
    pg, gi, og = pl.pallas_call(
        add_kernel,
        out_shape=(
            jax.ShapeDtypeStruct((OWN,) + block, BF),
            jax.ShapeDtypeStruct((8, 8192), BF),
            jax.ShapeDtypeStruct((128, HS), BF),
        ),
        in_specs=[hb] * 4,
        out_specs=(hb, hb, hb),
        scratch_shapes=[
            pltpu.SMEM((2 * OWN,), jnp.int32),
            pltpu.VMEM((2 * OWN,) + block, BF),
            pltpu.VMEM((OWN,) + block, F32),
            pltpu.VMEM((OWN,) + block, BF),
            pltpu.VMEM((8, 8192), BF),
            pltpu.VMEM((128, HS), BF),
            dma((11,)),
        ],
        compiler_params=pltpu.CompilerParams(vmem_limit_bytes=60 * 1024 * 1024),
        name="add_returns",
    )(tab, ret, gi, og)
    return gi, pg.reshape((OWN, 1) + block), og.reshape(128, 1, HS)


def solution(mesh):
    placed = (
        P("owner", "tp"),
        P("owner", "tp"),
        P("owner", "tp", None),
        P("owner", "tp", None, None),
        P(None, "tp"),
        P(),
        P(),
        P(),
    )
    return jax.shard_map(
        body,
        mesh=mesh,
        in_specs=placed,
        out_specs=(P(("owner", "tp"), None), P("owner", "tp", None, None), P("owner", "tp", None)),
        check_vma=False,
    )
```
